256 devices in a mesh: ctx: 16 (over z, y_hi), head: 16 (over y_lo, x, core).
Axes of the slice: x: 4, y: 4 (y_hi: 2, y_lo: 2; y = y_hi * 2 + y_lo), z: 8, core: 2. Of those that a mesh axis runs over, the one named last changes fastest.
Arguments:
- asker_vectors: bfloat16 [4096, 64, 128], P('ctx', 'head'), may hold values from -15 to 15
- asker_memory_pairs: bfloat16 [4096, 16, 128], P('ctx'), may hold values from -9 to 9
- leading_memory_pairs: bfloat16 [1024, 16, 128], P('ctx'), may hold values from -9 to 9
- document_memory_pairs: bfloat16 [16384, 16, 128], P(('ctx', 'head')), may hold values from -200 to 200
- document_valid_extent: int32 [64], replicated, may hold values from 1 to 256, as said below
- softening_factor: float32 [64], P('head'), may hold values from 0.5 to 1
Outputs:
- attended: bfloat16 [4096, 64, 128], P('ctx', 'head')
The draws below stay inside these ranges and needn't reach their ends.
Inputs may be any that keep to these rules, and one draw needn't show every extreme that they name: `document_valid_extent`: passages are padded to tiles of 256 rows: each tile is full or is the last tile of a passage; tile 0 is full.
All inputs are finite; a program needn't handle non-finite values.
Results may differ from the reference program's by a relative error of at most 0.0045.
Values may be sent and summed in bfloat16 or wider, within the bound.
No kernel may reach another device: no remote copies, remote signals or barrier semaphores. Data moves between devices by JAX's collectives and lax.ppermute only.
A program may use at most 64 MiB of HBM per device.

```python
import math
import jax
import jax.numpy as jnp
from jax import lax

ASKER_COUNT = 64
KVH = 8
HD = 128
TILE = 256
PREFIX = 1024
QTOKENS = 4096
PASSAGE = 16384
TILES = 64


def draw_document_memory_pairs(key, part):
    key = jax.random.fold_in(key, 11)
    key_base = jax.random.fold_in(key, 0)
    shape = (PASSAGE, 2 * KVH, HD)
    values_all = jnp.clip(1.5 * jax.random.normal(key_base, shape, jnp.float32), -9.0, 9.0)
    return values_all.astype(jnp.bfloat16)


def draw_document_valid_extent(key, part):
    key = jax.random.fold_in(key, 5)
    key_len, key_last = jax.random.split(key)
    partial_len = jax.random.randint(key_len, (TILES,), 1, TILE + 1)
    is_last = jax.random.randint(key_last, (TILES,), 0, 3) == 0
    lengths = jnp.where(is_last, partial_len, TILE)
    return lengths.at[0].set(TILE).astype(jnp.int32)


def block_levels(stream_key, shape, pieces, low, largest):
    loudness = 1.0
    for dim, blocks in pieces:
        draws = jax.random.uniform(jax.random.fold_in(jax.random.fold_in(stream_key, 6), dim), (blocks,), jnp.float32, low / len(pieces), largest / len(pieces))
        loudness = loudness * jnp.repeat(jnp.exp(draws), shape[dim] // blocks).reshape((-1,) + (1,) * (len(shape) - 1 - dim))
    return loudness


def noise(stream_key, dims, spread, bound, cuts=(), kind=jnp.bfloat16):
    gain = block_levels(stream_key, dims, cuts, -0.22, 0.18) if cuts else 1.0
    result = jax.random.normal(stream_key, dims, jnp.float32) * spread * gain
    return jnp.minimum(jnp.maximum(result, -bound), bound).astype(kind)


def setup_inputs(seed: int = 0) -> dict:
    seeds = jax.random.split(jax.random.key(seed), 7)
    asker_vectors = noise(seeds[0], (QTOKENS, ASKER_COUNT, HD), 2.5, 15.0, ((0, 16), (1, 16)))
    asker_memory_pairs = noise(seeds[1], (QTOKENS, 2 * KVH, HD), 1.5, 9.0, ((0, 16),))
    leading_memory_pairs = noise(seeds[2], (PREFIX, 2 * KVH, HD), 1.5, 9.0, ((0, 16),))
    document_memory_pairs = draw_document_memory_pairs(jax.random.fold_in(seeds[6], 71), 0)
    document_valid_extent = draw_document_valid_extent(jax.random.fold_in(seeds[6], 71), 0)
    softening_factor = jnp.clip(jnp.exp(math.log(1.0) - 0.6931472 * jax.random.uniform(seeds[5], (ASKER_COUNT,), jnp.float32) ** block_levels(seeds[5], (ASKER_COUNT,), ((0, 16),), -0.2, 0.2)), 0.5, 1.0)
    return {"asker_vectors": asker_vectors, "asker_memory_pairs": asker_memory_pairs, "leading_memory_pairs": leading_memory_pairs, "document_memory_pairs": document_memory_pairs, "document_valid_extent": document_valid_extent, "softening_factor": softening_factor}


MASKED_SCORE = -1e+30

def reference(asker_vectors, asker_memory_pairs, leading_memory_pairs, document_memory_pairs, document_valid_extent, softening_factor):
    reciprocal_sqrt_dimension = 1.0 / math.sqrt(HD)
    askers_sharing_memory = ASKER_COUNT // KVH
    live = jnp.arange(PASSAGE) % TILE < jnp.repeat(document_valid_extent, TILE)
    causal = jnp.arange(QTOKENS)[:, None] >= jnp.arange(QTOKENS)[None, :]

    def solitary_channel(inputs):
        query_head, kv_head, head_temp = inputs
        key_slot = 2 * kv_head

        def scored(cache, factor):
            key_rows = jnp.take(cache, key_slot, axis=1)
            return jnp.dot(query_head, key_rows.T, preferred_element_type=jnp.float32) * factor

        def mixed(weights, cache):
            value_rows = jnp.take(cache, key_slot + 1, axis=1)
            return jnp.dot(weights.astype(jnp.bfloat16), value_rows, preferred_element_type=jnp.float32)
        pre_scores = scored(leading_memory_pairs, reciprocal_sqrt_dimension)
        pas_scores = jnp.where(live[None, :], scored(document_memory_pairs, reciprocal_sqrt_dimension / head_temp), MASKED_SCORE)
        qry_scores = jnp.where(causal, scored(asker_memory_pairs, reciprocal_sqrt_dimension), MASKED_SCORE)
        peak_row = jnp.maximum(jnp.maximum(pre_scores.max(axis=1), pas_scores.max(axis=1)), qry_scores.max(axis=1))[:, None]
        pre_weights = jnp.exp(pre_scores - peak_row)
        pas_weights = jnp.where(live[None, :], jnp.exp(pas_scores - peak_row), 0.0)
        qry_weights = jnp.where(causal, jnp.exp(qry_scores - peak_row), 0.0)
        total_row = pre_weights.sum(axis=1) + pas_weights.sum(axis=1) + qry_weights.sum(axis=1)
        summed = mixed(pre_weights, leading_memory_pairs) + mixed(pas_weights, document_memory_pairs) + mixed(qry_weights, asker_memory_pairs)
        return (summed / total_row[:, None]).astype(jnp.bfloat16)
    attended_results = lax.map(solitary_channel, (asker_vectors.transpose(1, 0, 2), jnp.arange(ASKER_COUNT) // askers_sharing_memory, softening_factor))
    return attended_results.transpose(1, 0, 2)
```

```python
import functools
import math

import jax
import jax.numpy as jnp
from jax import lax
from jax.experimental import pallas as pl
from jax.experimental.pallas import tpu as pltpu
from jax.sharding import Mesh
from jax.sharding import PartitionSpec as P

F32 = jnp.float32
BF16 = jnp.bfloat16
KVH = 8
HD = 128
TILE = 256
RING = 8
SEND = 64
ROWS = 1024
BLOCKS = 4
AUX = 16
SUB = 512
MASKED = -1e30
HEADROOM = 100.0
LOG2E = math.log2(math.e)
SCALE2 = LOG2E / math.sqrt(HD)
VMEM_LIMIT = 48 * 2**20


def shift(count, step):
    return [(i, (i + step) % count) for i in range(count)]


def params():
    return pltpu.CompilerParams(vmem_limit_bytes=VMEM_LIMIT)


def whole(shape):
    return pl.BlockSpec(shape, lambda *_: (0,) * len(shape))


def split3(x):
    hi = x.astype(BF16)
    rest = x - hi.astype(F32)
    mid = rest.astype(BF16)
    low = (rest - mid.astype(F32)).astype(BF16)
    return hi, mid, low


def join3(rows):
    r = rows.astype(F32)
    return r[0:1] + r[1:2] + r[2:3]


def aux_rows(x):
    hi, mid, low = split3(x)
    pad = jnp.zeros((AUX - 3, x.shape[1]), F32)
    parts = [hi.astype(F32), mid.astype(F32), low.astype(F32), pad]
    return jnp.concatenate(parts, axis=0).astype(BF16)


def prepare_queries(soft_ref, q_ref, out_ref):
    tokens, heads, _ = q_ref.shape
    for h in range(heads):
        cols = slice(h * tokens, (h + 1) * tokens)
        out_ref[:HD, cols] = q_ref[:, h, :].astype(F32).T.astype(BF16)
        factor = jnp.full((1, tokens), 1.0, F32) / soft_ref[h] * SCALE2
        out_ref[HD:, cols] = aux_rows(factor)


def query_block(asker_vectors, softening_factor):
    tokens, heads, _ = asker_vectors.shape
    return pl.pallas_call(
        prepare_queries,
        in_specs=[pl.BlockSpec(memory_space=pltpu.SMEM), pl.BlockSpec(memory_space=pltpu.VMEM)],
        out_shape=jax.ShapeDtypeStruct((HD + AUX, tokens * heads), BF16),
        compiler_params=params(),
        name="queries",
    )(softening_factor, asker_vectors)


def prepare_documents(live_ref, doc_ref, out_ref):
    rows = doc_ref.shape[0]
    keep = lax.broadcasted_iota(jnp.int32, (rows, HD), 0) < live_ref[0]
    for g in range(KVH):
        for s in range(2):
            out_ref[g, s] = jnp.where(keep, doc_ref[:, 2 * g + s, :].astype(F32), 0.0).astype(BF16)


def document_blocks(document_memory_pairs, live_count):
    rows = document_memory_pairs.shape[0]
    return pl.pallas_call(
        prepare_documents,
        in_specs=[pl.BlockSpec(memory_space=pltpu.SMEM), pl.BlockSpec(memory_space=pltpu.VMEM)],
        out_shape=jax.ShapeDtypeStruct((KVH, 2, rows, HD), BF16),
        compiler_params=params(),
        name="documents",
    )(live_count.reshape(1), document_memory_pairs)


def lazy_pass(k_ref, v_ref, q_ref, scores_of, m, l, acc, out):
    m_out, l_out, acc_out = out
    width = q_ref.shape[1]
    excess = None
    for i in range(width // SUB):
        cols = slice(i * SUB, (i + 1) * SUB)
        s = scores_of(jnp.dot(k_ref[...], q_ref[:HD, cols], preferred_element_type=F32), cols)
        base = m[:, cols]
        over = jnp.max(s, axis=0, keepdims=True) - base
        excess = over if excess is None else jnp.maximum(excess, over)
        p = jnp.exp2(s - base).astype(BF16)
        o = jnp.dot(v_ref[...], p, preferred_element_type=F32)
        m_out[:, cols] = base
        l_out[:, cols] = l[:, cols] + o[HD : HD + 1]
        acc_out[:, cols] = acc[:, cols] + o[:HD]
    return jnp.max(excess) > HEADROOM


def exact_pass(k_ref, v_ref, q_ref, scores_of, m, l, acc, out):
    m_out, l_out, acc_out = out

    def step(i, carry):
        cols = pl.ds(pl.multiple_of(i * 128, 128), 128)
        s = scores_of(jnp.dot(k_ref[...], q_ref[:HD, cols], preferred_element_type=F32), cols)
        base = m[:, cols]
        peak = jnp.maximum(base, jnp.max(s, axis=0, keepdims=True))
        shrink = jnp.exp2(base - peak)
        p = jnp.exp2(s - peak).astype(BF16)
        o = jnp.dot(v_ref[...], p, preferred_element_type=F32)
        m_out[:, cols] = peak
        l_out[:, cols] = l[:, cols] * shrink + o[HD : HD + 1]
        acc_out[:, cols] = acc[:, cols] * shrink + o[:HD]
        return carry

    lax.fori_loop(0, q_ref.shape[1] // 128, step, 0)


def passage_kernel(shards, first, *refs):
    refs = list(refs)
    q_ref = refs.pop(0)
    if first:
        pre_ref = refs.pop(0)
        m0, l0, acc0 = refs[-3:]
        refs = refs[:-3]
    else:
        m0, l0, acc0 = refs[:3]
        refs = refs[3:]
    pay = refs[:shards]
    live = refs[shards : 2 * shards]
    m_out, l_out, acc_out, k_ref, v_ref = refs[2 * shards :]

    @pl.when(pl.program_id(0) == 0)
    def _():
        at = 0
        for r, lv in zip(pay, live):
            span = r.shape[0] * SEND
            values = []
            for j in range(r.shape[0]):
                k_ref[at + j * SEND : at + (j + 1) * SEND, :] = r[j, 0]
                values.append(r[j, 1])
            stacked = jnp.concatenate(values, axis=0).astype(F32)
            v_ref[:HD, at : at + span] = stacked.T.astype(BF16)
            v_ref[HD:, at : at + span] = lv[...]
            at += span

    if first:
        s = jnp.dot(pre_ref[...], q_ref[:HD, :], preferred_element_type=F32) * SCALE2
        m0[...] = jnp.max(s, axis=0, keepdims=True)
        l0[...] = jnp.zeros_like(l0)
        acc0[...] = jnp.zeros_like(acc0)

    def factor(cols):
        return join3(q_ref[HD : HD + 3, cols])

    out = (m_out, l_out, acc_out)
    redo = lazy_pass(k_ref, v_ref, q_ref, lambda s, cols: s * factor(cols), m0, l0, acc0, out)

    @pl.when(redo)
    def _():
        count = k_ref.shape[0]
        alive = jnp.broadcast_to(v_ref[HD : HD + 1, :].astype(F32), (128, count)).T

        def scores(s, cols):
            return jnp.where(alive > 0.5, s * factor(cols), MASKED)

        exact_pass(k_ref, v_ref, q_ref, scores, m0, l0, acc0, out)


def state_shapes(width):
    return [
        jax.ShapeDtypeStruct((1, width), F32),
        jax.ShapeDtypeStruct((1, width), F32),
        jax.ShapeDtypeStruct((HD, width), F32),
    ]


def row_spec(height):
    return pl.BlockSpec((height, ROWS), lambda i: (0, i))


def state_specs():
    return [row_spec(1), row_spec(1), row_spec(HD)]


def passages(queries, state, pays, lives, prefix_keys=None):
    first = state is None
    width = queries.shape[1]
    keys = sum(p.shape[0] * SEND for p in pays)
    args = [queries]
    specs = [row_spec(HD + AUX)]
    scratch = [pltpu.VMEM((keys, HD), BF16), pltpu.VMEM((HD + AUX, keys), BF16)]
    if first:
        args.append(prefix_keys)
        specs.append(whole(prefix_keys.shape))
        scratch += [pltpu.VMEM((1, ROWS), F32), pltpu.VMEM((1, ROWS), F32), pltpu.VMEM((HD, ROWS), F32)]
    else:
        args += list(state)
        specs += state_specs()
    args += list(pays) + list(lives)
    specs += [whole(p.shape) for p in pays] + [whole(v.shape) for v in lives]
    return pl.pallas_call(
        functools.partial(passage_kernel, len(pays), first),
        grid=(width // ROWS,),
        in_specs=specs,
        out_specs=state_specs(),
        out_shape=state_shapes(width),
        scratch_shapes=scratch,
        compiler_params=params(),
        name="passages",
    )(*args)


def direct_kernel(info_ref, q_ref, m0, l0, acc0, cache_ref, m_out, l_out, acc_out, k_ref, v_ref):
    pre = cache_ref.shape[2] - 128
    block = pl.program_id(0)

    @pl.when(block == 0)
    def _():
        values = []
        for z in range(RING):
            k_ref[z * 128 : (z + 1) * 128, :] = cache_ref[z, 0, :128]
            k_ref[RING * 128 + z * pre : RING * 128 + (z + 1) * pre, :] = cache_ref[z, 0, 128:]
        for z in range(RING):
            values.append(cache_ref[z, 1, :128])
        for z in range(RING):
            values.append(cache_ref[z, 1, 128:])
        stacked = jnp.concatenate(values, axis=0).astype(F32)
        v_ref[:HD, :] = stacked.T.astype(BF16)
        v_ref[HD:, :] = jnp.ones((AUX, v_ref.shape[1]), BF16)

    zpos, ypos, cpos = info_ref[0], info_ref[1], info_ref[2]
    tokens = TILE
    yrow = jnp.where(block % 2 == 0, ypos, 1 - ypos)
    asked = RING * 128

    def scores(s, cols):
        n = s.shape[1]
        if isinstance(cols, slice):
            start = cols.start
        else:
            start = cols.start
        token = (lax.broadcasted_iota(jnp.int32, (1, n), 1) + start) % tokens
        query = (2 * zpos + yrow) * tokens + token
        row = lax.broadcasted_iota(jnp.int32, (asked, 1), 0)
        key = (2 * (row // 128) + ypos) * tokens + cpos * 128 + row % 128
        s = s * SCALE2
        head = jnp.where(key <= query, s[:asked], MASKED)
        return jnp.concatenate([head, s[asked:]], axis=0)

    out = (m_out, l_out, acc_out)
    redo = lazy_pass(k_ref, v_ref, q_ref, scores, m0, l0, acc0, out)

    @pl.when(redo)
    def _():
        exact_pass(k_ref, v_ref, q_ref, scores, m0, l0, acc0, out)


def direct(queries, state, cache, info):
    width = queries.shape[1]
    keys = cache.shape[0] * cache.shape[2]
    return pl.pallas_call(
        direct_kernel,
        grid=(width // ROWS,),
        in_specs=[pl.BlockSpec(memory_space=pltpu.SMEM), row_spec(HD + AUX)] + state_specs() + [whole(cache.shape)],
        out_specs=state_specs(),
        out_shape=state_shapes(width),
        scratch_shapes=[pltpu.VMEM((keys, HD), BF16), pltpu.VMEM((HD + AUX, keys), BF16)],
        compiler_params=params(),
        name="direct",
    )(info, queries, *state, cache)


def pack(m, l, acc):
    total = m + jnp.log2(l)
    return jnp.concatenate([(acc / l).astype(BF16), aux_rows(total)], axis=0)


def pack_kernel(m, l, acc, out_ref):
    out_ref[...] = pack(m[...], l[...], acc[...])


def pack_blocks(state, low, high):
    width = (high - low) * ROWS

    def spec(height):
        return pl.BlockSpec((height, ROWS), lambda i: (0, i + low))

    return pl.pallas_call(
        pack_kernel,
        grid=(high - low,),
        in_specs=[spec(1), spec(1), spec(HD)],
        out_specs=row_spec(HD + AUX),
        out_shape=jax.ShapeDtypeStruct((HD + AUX, width), BF16),
        compiler_params=params(),
        name="pack",
    )(*state)


def fold(m, l, acc, received):
    other = join3(received[HD : HD + 3])
    peak = jnp.maximum(m, other)
    mine = jnp.exp2(m - peak)
    theirs = jnp.exp2(other - peak)
    return peak, l * mine + theirs, acc * mine + received[:HD].astype(F32) * theirs


def merge_kernel(m, l, acc, rec, m_out, l_out, acc_out, send_ref):
    total = m[...] + jnp.log2(l[...])
    m1, l1, acc1 = fold(total, jnp.ones_like(total), acc[...] / l[...], rec[...])

    @pl.when(pl.program_id(0) == 0)
    def _():
        send_ref[...] = pack(m1, l1, acc1)

    @pl.when(pl.program_id(0) == 1)
    def _():
        m_out[...] = m1
        l_out[...] = l1
        acc_out[...] = acc1


def merge_cores(state, received):
    def spec(height):
        return pl.BlockSpec((height, ROWS), lambda i: (0, 1 - i))

    def fixed(height):
        return pl.BlockSpec((height, ROWS), lambda i: (0, 0))

    return pl.pallas_call(
        merge_kernel,
        grid=(2,),
        in_specs=[spec(1), spec(1), spec(HD), spec(HD + AUX)],
        out_specs=[fixed(1), fixed(1), fixed(HD), fixed(HD + AUX)],
        out_shape=state_shapes(ROWS) + [jax.ShapeDtypeStruct((HD + AUX, ROWS), BF16)],
        compiler_params=params(),
        name="merge",
    )(*state, received)


def finish_kernel(m, l, acc, rec, out_ref):
    _, l1, acc1 = fold(m[...], l[...], acc[...], rec[...])
    result = acc1 / l1
    tokens, heads, _ = out_ref.shape
    for h in range(heads):
        out_ref[:, h, :] = result[:, h * tokens : (h + 1) * tokens].T.astype(BF16)


def finish(state, received, shape):
    return pl.pallas_call(
        finish_kernel,
        out_shape=jax.ShapeDtypeStruct(shape, BF16),
        compiler_params=params(),
        name="finish",
    )(*state, received)


def body(
    asker_vectors,
    asker_memory_pairs,
    leading_memory_pairs,
    document_memory_pairs,
    document_valid_extent,
    softening_factor,
):
    zpos, ypos, cpos = lax.axis_index("z"), lax.axis_index("yh"), lax.axis_index("c")
    group = lax.axis_index("yl") * 4 + lax.axis_index("x")
    ctx = 2 * zpos + ypos

    extent = document_valid_extent.reshape(RING, 2, 4)
    extent = lax.dynamic_index_in_dim(extent, ypos, 1, keepdims=False)
    offset = jnp.arange(2, dtype=jnp.int32) * 128 + cpos * SEND
    counts = (extent[:, :, None] - offset[None, None, :]).reshape(RING, KVH)
    counts = jnp.roll(counts, -zpos, axis=0)
    live = jnp.arange(SEND, dtype=jnp.int32)[None, None, :] < counts[:, :, None]
    live = live.astype(BF16).reshape(RING, 1, KVH * SEND)
    live = jnp.broadcast_to(live, (RING, AUX, KVH * SEND))
    own_count = lax.dynamic_index_in_dim(counts[0], group, 0, keepdims=False)

    sending = document_blocks(document_memory_pairs, own_count)
    own = lax.all_to_all(sending, ("yl", "x"), 0, 0, tiled=True)

    q0 = query_block(asker_vectors, softening_factor)
    q1 = lax.ppermute(q0, "yh", shift(2, 1))
    q2 = lax.ppermute(q0, "c", shift(2, 1))
    q3 = lax.ppermute(q1, "c", shift(2, 1))
    queries = jnp.concatenate([q0, q1, q2, q3], axis=1)

    half = asker_memory_pairs.shape[0] // 2
    lead = leading_memory_pairs.shape[0] // 2
    mine = lax.dynamic_slice(asker_memory_pairs, (cpos * half, 2 * group, 0), (half, 2, HD))
    led = lax.dynamic_slice(leading_memory_pairs, (cpos * lead, 2 * group, 0), (lead, 2, HD))
    cache_own = jnp.concatenate([mine, led], axis=0).transpose(1, 0, 2)
    cache = lax.all_gather(cache_own, "z", axis=0, tiled=False)
    prefix_keys = cache_own[0, half:]

    up, down = shift(RING, 1), shift(RING, -1)
    f1 = lax.ppermute(own, "z", up)
    b1 = lax.ppermute(own, "z", down)
    state = passages(queries, None, [own], [live[0]], prefix_keys)
    info = jnp.stack([zpos, ypos, cpos]).astype(jnp.int32)
    state = direct(queries, state, cache, info)
    f2 = lax.ppermute(f1, "z", up)
    b2 = lax.ppermute(b1, "z", down)
    state = passages(queries, state, [f1, b1], [live[7], live[1]])
    f3 = lax.ppermute(f2, "z", up)
    b3 = lax.ppermute(b2, "z", down)
    state = passages(queries, state, [f2, b2], [live[6], live[2]])
    f4 = lax.ppermute(f3[:4], "z", up)
    b4 = lax.ppermute(b3[4:], "z", down)
    state = passages(queries, state, [f3, b3], [live[5], live[3]])
    far = live[4]
    state = passages(queries, state, [f4, b4], [far[:, :256], far[:, 256:]])

    received = lax.ppermute(pack_blocks(state, 2, 4), "c", shift(2, 1))
    *kept, send = merge_cores(state, received)
    last = lax.ppermute(send, "yh", shift(2, 1))
    return finish(kept, last, asker_vectors.shape)


def solution(mesh):
    fine = Mesh(mesh.devices.reshape(8, 2, 2, 4, 2), ("z", "yh", "yl", "x", "c"))
    ctx, head = ("z", "yh"), ("yl", "x", "c")
    return jax.shard_map(
        body,
        mesh=fine,
        in_specs=(
            P(ctx, head, None),
            P(ctx, None, None),
            P(ctx, None, None),
            P(ctx + head, None, None),
            P(),
            P(head),
        ),
        out_specs=P(ctx, head, None),
        check_vma=False,
    )
```

```python
import functools
import math

import jax
import jax.numpy as jnp
from jax import lax
from jax.experimental import pallas as pl
from jax.experimental.pallas import tpu as pltpu
from jax.sharding import Mesh
from jax.sharding import PartitionSpec as P

F32 = jnp.float32
BF16 = jnp.bfloat16
KVH = 8
HD = 128
TILE = 256
RING = 8
SEND = 64
ROWS = 1024
BLOCKS = 4
AUX = 16
ASKED = 128
LED = 32
CACHE_ROWS = 2 * (ASKED + LED)
UNROLL = 2
SUB = 512
MASKED = -1e30
HEADROOM = 100.0
LOG2E = math.log2(math.e)
SCALE2 = LOG2E / math.sqrt(HD)
VMEM_LIMIT = 24 * 2**20


def shift(count, step):
    return [(i, (i + step) % count) for i in range(count)]


def params():
    return pltpu.CompilerParams(vmem_limit_bytes=VMEM_LIMIT)


def whole(shape):
    return pl.BlockSpec(shape, lambda *_: (0,) * len(shape))


def after(x, *others):
    return lax.optimization_barrier((x, *others))[0]


def split3(x):
    hi = x.astype(BF16)
    rest = x - hi.astype(F32)
    mid = rest.astype(BF16)
    low = (rest - mid.astype(F32)).astype(BF16)
    return hi, mid, low


def join3(rows):
    r = rows.astype(F32)
    return r[0:1] + r[1:2] + r[2:3]


def aux_rows(x):
    hi, mid, low = split3(x)
    pad = jnp.zeros((AUX - 3, x.shape[1]), F32)
    parts = [hi.astype(F32), mid.astype(F32), low.astype(F32), pad]
    return jnp.concatenate(parts, axis=0).astype(BF16)


def prepare_queries(soft_ref, q_ref, out_ref):
    tokens, heads, _ = q_ref.shape
    for h in range(heads):
        cols = slice(h * tokens, (h + 1) * tokens)
        out_ref[:HD, cols] = q_ref[:, h, :].astype(F32).T.astype(BF16)
        factor = jnp.full((1, tokens), 1.0, F32) / soft_ref[h] * SCALE2
        out_ref[HD:, cols] = aux_rows(factor)


def query_block(asker_vectors, softening_factor):
    tokens, heads, _ = asker_vectors.shape
    return pl.pallas_call(
        prepare_queries,
        in_specs=[pl.BlockSpec(memory_space=pltpu.SMEM), pl.BlockSpec(memory_space=pltpu.VMEM)],
        out_shape=jax.ShapeDtypeStruct((HD + AUX, tokens * heads), BF16),
        compiler_params=params(),
        name="queries",
    )(softening_factor, asker_vectors)


def live_counts(extent_ref, zpos):
    base = (2 * zpos + lax.axis_index("yh")) * 4
    start = lax.axis_index("c") * SEND
    return [extent_ref[base + j // 2] - (j % 2) * 128 - start for j in range(KVH)]


def prepare_documents(extent_ref, doc_ref, out_ref):
    rows = doc_ref.shape[0]
    own = lax.axis_index("yl") * 4 + lax.axis_index("x")
    live = jnp.int32(0)
    for j, count in enumerate(live_counts(extent_ref, lax.axis_index("z"))):
        live = jnp.where(own == j, count, live)
    keep = lax.broadcasted_iota(jnp.int32, (rows, HD), 0) < live
    for g in range(KVH):
        for s in range(2):
            out_ref[g, s] = jnp.where(keep, doc_ref[:, 2 * g + s, :].astype(F32), 0.0).astype(BF16)


def document_blocks(document_memory_pairs, extent):
    rows = document_memory_pairs.shape[0]
    return pl.pallas_call(
        prepare_documents,
        in_specs=[pl.BlockSpec(memory_space=pltpu.SMEM), pl.BlockSpec(memory_space=pltpu.VMEM)],
        out_shape=jax.ShapeDtypeStruct((KVH, 2, rows, HD), BF16),
        compiler_params=params(),
        name="documents",
    )(extent, document_memory_pairs)


def prepare_caches(asker_ref, lead_ref, out_ref):
    own = lax.axis_index("yl") * 4 + lax.axis_index("x")
    c = lax.axis_index("c")
    half, lead = asker_ref.shape[0] // 2, lead_ref.shape[0] // 2
    mine = pl.ds(pl.multiple_of(c * half, half), half)
    led = pl.ds(pl.multiple_of(c * lead, lead), lead)
    for g in range(KVH):

        @pl.when(own == g)
        def _():
            for s in range(2):
                out_ref[s * half : (s + 1) * half, :] = asker_ref[mine, 2 * g + s, :]
                at = 2 * half + s * lead
                out_ref[at : at + lead, :] = lead_ref[led, 2 * g + s, :]


def cache_block(asker_memory_pairs, leading_memory_pairs):
    return pl.pallas_call(
        prepare_caches,
        out_shape=jax.ShapeDtypeStruct((CACHE_ROWS, HD), BF16),
        compiler_params=params(),
        name="caches",
    )(asker_memory_pairs, leading_memory_pairs)


def attend_kernel(shards, first, *refs):
    refs = list(refs)
    extent_ref, q_ref = refs[:2]
    refs = refs[2:]
    if first:
        m0, l0, acc0 = refs[-3:]
        refs = refs[:-3]
    else:
        m0, l0, acc0 = refs[:3]
        refs = refs[3:]
    pay = refs[: len(shards)]
    m_out, l_out, acc_out, k_ref, v_ref = refs[len(shards) :]
    width = q_ref.shape[1]
    count = len(shards)
    zpos, ypos, cpos = lax.axis_index("z"), lax.axis_index("yh"), lax.axis_index("c")
    span = KVH * SEND
    asked_at = count * span
    led_at = asked_at + count * ASKED

    values, asked, led, alive, asked_alive = [], [], [], [], []
    for n, (ref, away) in enumerate(zip(pay, shards)):
        counts = live_counts(extent_ref, (zpos + away) % RING)
        lane = lax.broadcasted_iota(jnp.int32, (AUX, span), 1)
        bound = jnp.zeros((AUX, span), jnp.int32)
        for j in range(KVH):
            bound = jnp.where(lane // SEND == j, counts[j], bound)
            at = n * span + j * SEND
            k_ref[at : at + SEND, :] = ref[2 * j * SEND : (2 * j + 1) * SEND, :]
            values.append(ref[(2 * j + 1) * SEND : (2 * j + 2) * SEND, :])
        alive.append(jnp.where(lane % SEND < bound, 1.0, 0.0))
        at = 2 * span
        keys = ref[at : at + ASKED, :]
        vals = ref[at + ASKED : at + 2 * ASKED, :]
        if away == 0:
            asked_alive.append(jnp.ones((AUX, ASKED), F32))
        else:
            seen = (zpos + away >= 0) if away < 0 else (zpos + away >= RING)
            flag = jnp.where(seen, 1.0, 0.0).astype(F32)
            keys = (keys.astype(F32) * flag).astype(BF16)
            vals = (vals.astype(F32) * flag).astype(BF16)
            asked_alive.append(jnp.full((AUX, ASKED), 1.0, F32) * flag)
        k_ref[asked_at + n * ASKED : asked_at + (n + 1) * ASKED, :] = keys
        asked.append(vals)
        at += 2 * ASKED
        k_ref[led_at + n * LED : led_at + (n + 1) * LED, :] = ref[at : at + LED, :]
        led.append(ref[at + LED : at + 2 * LED, :])
    stacked = jnp.concatenate(values + asked + led, axis=0).astype(F32)
    v_ref[:HD, :] = stacked.T.astype(BF16)
    ones = [jnp.ones((AUX, count * LED), F32)]
    v_ref[HD:, :] = jnp.concatenate(alive + asked_alive + ones, axis=1).astype(BF16)

    if first:
        for i in range(width // SUB):
            cols = slice(i * SUB, (i + 1) * SUB)
            s = jnp.dot(k_ref[led_at:, :], q_ref[:HD, cols], preferred_element_type=F32) * SCALE2
            m0[:, cols] = jnp.max(s, axis=0, keepdims=True)
        l0[...] = jnp.zeros_like(l0)
        acc0[...] = jnp.zeros_like(acc0)

    def scores(cols, start, size):
        s = jnp.dot(k_ref[...], q_ref[:HD, cols], preferred_element_type=F32)
        factor = join3(q_ref[HD : HD + 3, cols])
        rest = s[asked_at:] * SCALE2
        if first:
            token = (lax.broadcasted_iota(jnp.int32, (1, size), 1) + start) % TILE
            block = start // ROWS
            yrow = jnp.where(block % 2 == 0, ypos, 1 - ypos)
            query = yrow * TILE + token
            key = ypos * TILE + cpos * ASKED + lax.broadcasted_iota(jnp.int32, (ASKED, 1), 0)
            near = jnp.where(key <= query, rest[:ASKED], MASKED)
            rest = jnp.concatenate([near, rest[ASKED:]], axis=0)
        return jnp.concatenate([s[:asked_at] * factor, rest], axis=0)

    def lazy(i, excess):
        start = pl.multiple_of(i * SUB, SUB)
        cols = pl.ds(start, SUB)
        s = scores(cols, start, SUB)
        base = m0[:, cols]
        excess = jnp.maximum(excess, jnp.max(s, axis=0, keepdims=True) - base)
        p = jnp.exp2(s - base).astype(BF16)
        o = jnp.dot(v_ref[...], p, preferred_element_type=F32)
        m_out[:, cols] = base
        l_out[:, cols] = l0[:, cols] + o[HD : HD + 1]
        acc_out[:, cols] = acc0[:, cols] + o[:HD]
        return excess

    excess = lax.fori_loop(0, width // SUB, lazy, jnp.full((1, SUB), MASKED, F32), unroll=UNROLL)

    @pl.when(jnp.max(excess) > HEADROOM)
    def _():
        total = k_ref.shape[0]
        living = jnp.broadcast_to(v_ref[HD : HD + 1, :].astype(F32), (128, total)).T

        def exact(i, carry):
            start = pl.multiple_of(i * 128, 128)
            cols = pl.ds(start, 128)
            s = jnp.where(living > 0.5, scores(cols, start, 128), MASKED)
            base = m0[:, cols]
            peak = jnp.maximum(base, jnp.max(s, axis=0, keepdims=True))
            shrink = jnp.exp2(base - peak)
            p = jnp.exp2(s - peak).astype(BF16)
            o = jnp.dot(v_ref[...], p, preferred_element_type=F32)
            m_out[:, cols] = peak
            l_out[:, cols] = l0[:, cols] * shrink + o[HD : HD + 1]
            acc_out[:, cols] = acc0[:, cols] * shrink + o[:HD]
            return carry

        lax.fori_loop(0, width // 128, exact, 0)


def state_shapes(width):
    return [
        jax.ShapeDtypeStruct((1, width), F32),
        jax.ShapeDtypeStruct((1, width), F32),
        jax.ShapeDtypeStruct((HD, width), F32),
    ]


def row_spec(height):
    return pl.BlockSpec((height, ROWS), lambda i: (0, i))


def attend(extent, queries, state, pays, shards):
    first = state is None
    width = queries.shape[1]
    keys = len(shards) * (KVH * SEND + ASKED + LED)
    scratch = [pltpu.VMEM((keys, HD), BF16), pltpu.VMEM((HD + AUX, keys), BF16)]
    args = [extent, queries]
    if first:
        scratch += [pltpu.VMEM((1, width), F32), pltpu.VMEM((1, width), F32), pltpu.VMEM((HD, width), F32)]
    else:
        args += list(state)
    args += list(pays)
    vmem = pl.BlockSpec(memory_space=pltpu.VMEM)
    return pl.pallas_call(
        functools.partial(attend_kernel, shards, first),
        in_specs=[pl.BlockSpec(memory_space=pltpu.SMEM)] + [vmem] * (len(args) - 1),
        out_specs=[vmem] * 3,
        out_shape=state_shapes(width),
        scratch_shapes=scratch,
        compiler_params=params(),
        name="attend",
    )(*args)


def pack(m, l, acc):
    total = m + jnp.log2(l)
    return jnp.concatenate([(acc / l).astype(BF16), aux_rows(total)], axis=0)


def pack_kernel(m, l, acc, out_ref):
    out_ref[...] = pack(m[...], l[...], acc[...])


def pack_blocks(state, low, high):
    width = (high - low) * ROWS

    def spec(height):
        return pl.BlockSpec((height, ROWS), lambda i: (0, i + low))

    return pl.pallas_call(
        pack_kernel,
        grid=(high - low,),
        in_specs=[spec(1), spec(1), spec(HD)],
        out_specs=row_spec(HD + AUX),
        out_shape=jax.ShapeDtypeStruct((HD + AUX, width), BF16),
        compiler_params=params(),
        name="pack",
    )(*state)


def fold(m, l, acc, received):
    other = join3(received[HD : HD + 3])
    peak = jnp.maximum(m, other)
    mine = jnp.exp2(m - peak)
    theirs = jnp.exp2(other - peak)
    return peak, l * mine + theirs, acc * mine + received[:HD].astype(F32) * theirs


def merge_kernel(m, l, acc, rec, m_out, l_out, acc_out, send_ref):
    total = m[...] + jnp.log2(l[...])
    m1, l1, acc1 = fold(total, jnp.ones_like(total), acc[...] / l[...], rec[...])

    @pl.when(pl.program_id(0) == 0)
    def _():
        send_ref[...] = pack(m1, l1, acc1)

    @pl.when(pl.program_id(0) == 1)
    def _():
        m_out[...] = m1
        l_out[...] = l1
        acc_out[...] = acc1


def merge_cores(state, received):
    def spec(height):
        return pl.BlockSpec((height, ROWS), lambda i: (0, 1 - i))

    def fixed(height):
        return pl.BlockSpec((height, ROWS), lambda i: (0, 0))

    return pl.pallas_call(
        merge_kernel,
        grid=(2,),
        in_specs=[spec(1), spec(1), spec(HD), spec(HD + AUX)],
        out_specs=[fixed(1), fixed(1), fixed(HD), fixed(HD + AUX)],
        out_shape=state_shapes(ROWS) + [jax.ShapeDtypeStruct((HD + AUX, ROWS), BF16)],
        compiler_params=params(),
        name="merge",
    )(*state, received)


def finish_kernel(m, l, acc, rec, out_ref):
    _, l1, acc1 = fold(m[...], l[...], acc[...], rec[...])
    result = acc1 / l1
    tokens, heads, _ = out_ref.shape
    for h in range(heads):
        out_ref[:, h, :] = result[:, h * tokens : (h + 1) * tokens].T.astype(BF16)


def finish(state, received, shape):
    return pl.pallas_call(
        finish_kernel,
        out_shape=jax.ShapeDtypeStruct(shape, BF16),
        compiler_params=params(),
        name="finish",
    )(*state, received)


def body(
    asker_vectors,
    asker_memory_pairs,
    leading_memory_pairs,
    document_memory_pairs,
    document_valid_extent,
    softening_factor,
):
    extent = document_valid_extent
    sending = document_blocks(document_memory_pairs, extent)
    q0 = query_block(after(asker_vectors, sending), softening_factor)
    q1 = lax.ppermute(q0, "yh", shift(2, 1))
    q2 = lax.ppermute(q0, "c", shift(2, 1))
    cache = cache_block(asker_memory_pairs, leading_memory_pairs)
    moved = lax.all_to_all(sending, ("yl", "x"), 0, 0, tiled=True)
    own = jnp.concatenate([moved.reshape(-1, HD), cache], axis=0)

    up, down = shift(RING, 1), shift(RING, -1)
    f1 = lax.ppermute(own, "z", up)
    b1 = lax.ppermute(own, "z", down)
    q3 = lax.ppermute(q1, "c", shift(2, 1))
    queries = jnp.concatenate([q0, q1, q2, q3], axis=1)
    state = attend(extent, queries, None, [own], [0])
    f2 = lax.ppermute(after(f1, state[0]), "z", up)
    b2 = lax.ppermute(after(b1, state[0]), "z", down)
    state = attend(extent, queries, state, [f1, b1], [-1, 1])
    f3 = lax.ppermute(after(f2, state[0]), "z", up)
    b3 = lax.ppermute(after(b2, state[0]), "z", down)
    state = attend(extent, queries, state, [f2, b2], [-2, 2])
    f4 = lax.ppermute(after(f3, state[0]), "z", up)
    state = attend(extent, queries, state, [f3, b3], [-3, 3])
    state = attend(extent, queries, state, [f4], [-4])

    received = lax.ppermute(pack_blocks(state, 2, 4), "c", shift(2, 1))
    *kept, send = merge_cores(state, received)
    last = lax.ppermute(send, "yh", shift(2, 1))
    return finish(kept, last, asker_vectors.shape)


def solution(mesh):
    fine = Mesh(mesh.devices.reshape(8, 2, 2, 4, 2), ("z", "yh", "yl", "x", "c"))
    ctx, head = ("z", "yh"), ("yl", "x", "c")
    return jax.shard_map(
        body,
        mesh=fine,
        in_specs=(
            P(ctx, head, None),
            P(ctx, None, None),
            P(ctx, None, None),
            P(ctx + head, None, None),
            P(),
            P(head),
        ),
        out_specs=P(ctx, head, None),
        check_vma=False,
    )
```

```python
import functools
import math

import jax
import jax.numpy as jnp
from jax import lax
from jax.experimental import pallas as pl
from jax.experimental.pallas import tpu as pltpu
from jax.sharding import Mesh
from jax.sharding import PartitionSpec as P

F32 = jnp.float32
BF16 = jnp.bfloat16
KVH = 8
HD = 128
TILE = 256
RING = 8
SEND = 64
ROWS = 1024
BLOCKS = 4
AUX = 16
ASKED = 128
LED = 32
CACHE_ROWS = 2 * (ASKED + LED)
UNROLL = 2
SUB = 1024
MASKED = -1e30
HEADROOM = 100.0
LOG2E = math.log2(math.e)
SCALE2 = LOG2E / math.sqrt(HD)
VMEM_LIMIT = 24 * 2**20


def shift(count, step):
    return [(i, (i + step) % count) for i in range(count)]


def params():
    return pltpu.CompilerParams(vmem_limit_bytes=VMEM_LIMIT)


def whole(shape):
    return pl.BlockSpec(shape, lambda *_: (0,) * len(shape))


def after(x, *others):
    return lax.optimization_barrier((x, *others))[0]


def split3(x):
    hi = x.astype(BF16)
    rest = x - hi.astype(F32)
    mid = rest.astype(BF16)
    low = (rest - mid.astype(F32)).astype(BF16)
    return hi, mid, low


def join3(rows):
    r = rows.astype(F32)
    return r[0:1] + r[1:2] + r[2:3]


def aux_rows(x):
    hi, mid, low = split3(x)
    pad = jnp.zeros((AUX - 3, x.shape[1]), F32)
    parts = [hi.astype(F32), mid.astype(F32), low.astype(F32), pad]
    return jnp.concatenate(parts, axis=0).astype(BF16)


def live_counts(extent_ref, zpos, cpos):
    base = (2 * zpos + lax.axis_index("yh")) * 4
    start = cpos * SEND
    return [extent_ref[base + j // 2] - (j % 2) * 128 - start for j in range(KVH)]


def prepare(extent_hbm, soft_hbm, doc_hbm, q_hbm, doc_out, q_out, extent_ref, soft_ref, doc_ref, q_ref, sems):
    pairs = ((extent_hbm, extent_ref), (doc_hbm, doc_ref), (soft_hbm, soft_ref), (q_hbm, q_ref))
    copies = [pltpu.make_async_copy(src, dst, sems.at[i]) for i, (src, dst) in enumerate(pairs)]
    for copy in copies:
        copy.start()
    copies[0].wait()
    copies[1].wait()
    rows = doc_ref.shape[0]
    own = lax.axis_index("yl") * 4 + lax.axis_index("x")
    live = jnp.int32(0)
    for j, count in enumerate(live_counts(extent_ref, lax.axis_index("z"), lax.axis_index("c"))):
        live = jnp.where(own == j, count, live)
    keep = lax.broadcasted_iota(jnp.int32, (rows, HD), 0) < live
    for g in range(KVH):
        for s in range(2):
            doc_out[g, s] = jnp.where(keep, doc_ref[:, 2 * g + s, :].astype(F32), 0.0).astype(BF16)
    copies[2].wait()
    copies[3].wait()
    tokens, heads, _ = q_ref.shape
    for h in range(heads):
        cols = slice(h * tokens, (h + 1) * tokens)
        q_out[:HD, cols] = q_ref[:, h, :].astype(F32).T.astype(BF16)
        factor = jnp.full((1, tokens), 1.0, F32) / soft_ref[h] * SCALE2
        q_out[HD:, cols] = aux_rows(factor)


def prepared(extent, softening_factor, document_memory_pairs, asker_vectors):
    rows = document_memory_pairs.shape[0]
    tokens, heads, _ = asker_vectors.shape
    vmem = pl.BlockSpec(memory_space=pltpu.VMEM)
    return pl.pallas_call(
        prepare,
        in_specs=[pl.BlockSpec(memory_space=pltpu.HBM)] * 4,
        out_specs=[vmem, vmem],
        out_shape=[
            jax.ShapeDtypeStruct((KVH, 2, rows, HD), BF16),
            jax.ShapeDtypeStruct((HD + AUX, tokens * heads), BF16),
        ],
        scratch_shapes=[
            pltpu.SMEM(extent.shape, jnp.int32),
            pltpu.SMEM(softening_factor.shape, F32),
            pltpu.VMEM(document_memory_pairs.shape, BF16),
            pltpu.VMEM(asker_vectors.shape, BF16),
            pltpu.SemaphoreType.DMA((4,)),
        ],
        compiler_params=params(),
        name="prepare",
    )(*[pltpu.with_memory_space_constraint(x, pltpu.HBM) for x in (extent, softening_factor, document_memory_pairs, asker_vectors)])


def prepare_caches(asker_ref, lead_ref, out_ref):
    own = lax.axis_index("yl") * 4 + lax.axis_index("x")
    c = lax.axis_index("c")
    half, lead = asker_ref.shape[0] // 2, lead_ref.shape[0] // 2
    mine = pl.ds(pl.multiple_of(c * half, half), half)
    led = pl.ds(pl.multiple_of(c * lead, lead), lead)
    for g in range(KVH):

        @pl.when(own == g)
        def _():
            for s in range(2):
                out_ref[s * half : (s + 1) * half, :] = asker_ref[mine, 2 * g + s, :]
                at = 2 * half + s * lead
                out_ref[at : at + lead, :] = lead_ref[led, 2 * g + s, :]


def cache_block(asker_memory_pairs, leading_memory_pairs):
    return pl.pallas_call(
        prepare_caches,
        out_shape=jax.ShapeDtypeStruct((CACHE_ROWS, HD), BF16),
        compiler_params=params(),
        name="caches",
    )(asker_memory_pairs, leading_memory_pairs)


def attend_kernel(shards, mode, q_low, *refs):
    refs = list(refs)
    extent_ref = refs.pop(0)
    first = mode == "first"
    count = len(shards)
    if first:
        parts = refs[:BLOCKS]
        pay = refs[BLOCKS : BLOCKS + count]
        m_out, l_out, acc_out, q_ref, k_ref, v_ref, m0, l0, acc0 = refs[BLOCKS + count :]
        for n, part in enumerate(parts):
            q_ref[:, n * ROWS : (n + 1) * ROWS] = part[...]
    else:
        q_ref, m0, l0, acc0 = refs[:4]
        pay = refs[4 : 4 + count]
        refs = refs[4 + count :]
        if mode in ("middle", "part"):
            m_out, l_out, acc_out, k_ref, v_ref = refs
        elif mode == "pack":
            m_out, l_out, acc_out, packed_ref, k_ref, v_ref = refs
        else:
            rec_ref, m_end, l_end, acc_end, k_ref, v_ref, m_out, l_out, acc_out = refs
    width = m_out.shape[1]
    zpos, ypos, cpos = lax.axis_index("z"), lax.axis_index("yh"), lax.axis_index("c")
    span = KVH * SEND
    asked_at = count * span
    led_at = asked_at + count * ASKED

    values, asked, led, alive, asked_alive = [], [], [], [], []
    for n, (ref, (away, swapped)) in enumerate(zip(pay, shards)):
        counts = live_counts(extent_ref, (zpos + away) % RING, 1 - cpos if swapped else cpos)
        lane = lax.broadcasted_iota(jnp.int32, (AUX, span), 1)
        bound = jnp.zeros((AUX, span), jnp.int32)
        for j in range(KVH):
            bound = jnp.where(lane // SEND == j, counts[j], bound)
            at = n * span + j * SEND
            k_ref[at : at + SEND, :] = ref[2 * j * SEND : (2 * j + 1) * SEND, :]
            values.append(ref[(2 * j + 1) * SEND : (2 * j + 2) * SEND, :])
        alive.append(jnp.where(lane % SEND < bound, 1.0, 0.0))
        at = 2 * span
        keys = ref[at : at + ASKED, :]
        vals = ref[at + ASKED : at + 2 * ASKED, :]
        if away == 0:
            asked_alive.append(jnp.ones((AUX, ASKED), F32))
        else:
            seen = (zpos + away >= 0) if away < 0 else (zpos + away >= RING)
            flag = jnp.where(seen, 1.0, 0.0).astype(F32)
            keys = (keys.astype(F32) * flag).astype(BF16)
            vals = (vals.astype(F32) * flag).astype(BF16)
            asked_alive.append(jnp.full((AUX, ASKED), 1.0, F32) * flag)
        k_ref[asked_at + n * ASKED : asked_at + (n + 1) * ASKED, :] = keys
        asked.append(vals)
        at += 2 * ASKED
        k_ref[led_at + n * LED : led_at + (n + 1) * LED, :] = ref[at : at + LED, :]
        led.append(ref[at + LED : at + 2 * LED, :])
    stacked = jnp.concatenate(values + asked + led, axis=0).astype(F32)
    v_ref[:HD, :] = stacked.T.astype(BF16)
    ones = [jnp.ones((AUX, count * LED), F32)]
    v_ref[HD:, :] = jnp.concatenate(alive + asked_alive + ones, axis=1).astype(BF16)

    if first:
        for i in range(width // SUB):
            cols = slice(i * SUB, (i + 1) * SUB)
            s = jnp.dot(k_ref[led_at:, :], q_ref[:HD, q_low + i * SUB : q_low + (i + 1) * SUB], preferred_element_type=F32) * SCALE2
            m0[:, cols] = jnp.max(s, axis=0, keepdims=True)
        l0[...] = jnp.zeros_like(l0)
        acc0[...] = jnp.zeros_like(acc0)

    def scores(start, size):
        cols = pl.ds(pl.multiple_of(start + q_low, 128), size)
        s = jnp.dot(k_ref[...], q_ref[:HD, cols], preferred_element_type=F32)
        factor = join3(q_ref[HD : HD + 3, cols])
        rest = s[asked_at:] * SCALE2
        if first:
            token = (lax.broadcasted_iota(jnp.int32, (1, size), 1) + start) % TILE
            yrow = jnp.where(start + q_low < 2 * ROWS, ypos, 1 - ypos)
            query = yrow * TILE + token
            key = ypos * TILE + cpos * ASKED + lax.broadcasted_iota(jnp.int32, (ASKED, 1), 0)
            near = jnp.where(key <= query, rest[:ASKED], MASKED)
            rest = jnp.concatenate([near, rest[ASKED:]], axis=0)
        return jnp.concatenate([s[:asked_at] * factor, rest], axis=0)

    def lazy(i, excess):
        start = pl.multiple_of(i * SUB, SUB)
        cols = pl.ds(start, SUB)
        old = pl.ds(pl.multiple_of(start + q_low, 128), SUB)
        s = scores(start, SUB)
        base = m0[:, old]
        excess = jnp.maximum(excess, jnp.max(s, axis=0, keepdims=True) - base)
        p = jnp.exp2(s - base).astype(BF16)
        o = jnp.dot(v_ref[...], p, preferred_element_type=F32)
        m_out[:, cols] = base
        l_out[:, cols] = l0[:, old] + o[HD : HD + 1]
        acc_out[:, cols] = acc0[:, old] + o[:HD]
        return excess

    excess = lax.fori_loop(0, width // SUB, lazy, jnp.full((1, SUB), MASKED, F32), unroll=min(UNROLL, width // SUB))

    @pl.when(jnp.max(excess) > HEADROOM)
    def _():
        total = k_ref.shape[0]
        living = jnp.broadcast_to(v_ref[HD : HD + 1, :].astype(F32), (128, total)).T

        def exact(i, carry):
            start = pl.multiple_of(i * 128, 128)
            cols = pl.ds(start, 128)
            old = pl.ds(pl.multiple_of(start + q_low, 128), 128)
            s = jnp.where(living > 0.5, scores(start, 128), MASKED)
            base = m0[:, old]
            peak = jnp.maximum(base, jnp.max(s, axis=0, keepdims=True))
            shrink = jnp.exp2(base - peak)
            p = jnp.exp2(s - peak).astype(BF16)
            o = jnp.dot(v_ref[...], p, preferred_element_type=F32)
            m_out[:, cols] = peak
            l_out[:, cols] = l0[:, old] * shrink + o[HD : HD + 1]
            acc_out[:, cols] = acc0[:, old] * shrink + o[:HD]
            return carry

        lax.fori_loop(0, width // 128, exact, 0)

    if mode == "pack":
        for n in range(2):
            cols = slice((2 * n + 1) * ROWS, (2 * n + 2) * ROWS)
            packed_ref[:, n * ROWS : (n + 1) * ROWS] = pack(m_out[:, cols], l_out[:, cols], acc_out[:, cols])
    if mode == "keep":
        m_end[...], l_end[...], acc_end[...] = fold(*normal(m_out[...], l_out[...], acc_out[...]), rec_ref[:, :ROWS])


def state_shapes(width):
    return [
        jax.ShapeDtypeStruct((1, width), F32),
        jax.ShapeDtypeStruct((1, width), F32),
        jax.ShapeDtypeStruct((HD, width), F32),
    ]


def attend(extent, queries, state, pays, shards, mode, received=None, q_low=0):
    keys = len(shards) * (KVH * SEND + ASKED + LED)
    width = ROWS if mode in ("part", "keep") else BLOCKS * ROWS
    scratch = [pltpu.VMEM((keys, HD), BF16), pltpu.VMEM((HD + AUX, keys), BF16)]
    floats = [pltpu.VMEM((1, width), F32), pltpu.VMEM((1, width), F32), pltpu.VMEM((HD, width), F32)]
    shapes = state_shapes(width)
    if mode == "first":
        args = [extent, *queries, *pays]
        shapes.append(jax.ShapeDtypeStruct((HD + AUX, width), BF16))
        scratch += floats
    else:
        args = [extent, queries, *state, *pays]
    if mode == "pack":
        shapes.append(jax.ShapeDtypeStruct((HD + AUX, 2 * ROWS), BF16))
    if mode == "keep":
        args.append(received)
        scratch += floats
    vmem = pl.BlockSpec(memory_space=pltpu.VMEM)
    return pl.pallas_call(
        functools.partial(attend_kernel, shards, mode, q_low),
        in_specs=[pl.BlockSpec(memory_space=pltpu.SMEM)] + [vmem] * (len(args) - 1),
        out_specs=[vmem] * len(shapes),
        out_shape=shapes,
        scratch_shapes=scratch,
        compiler_params=params(),
        name="attend",
    )(*args)


def pack(m, l, acc):
    total = m + jnp.log2(l)
    return jnp.concatenate([(acc / l).astype(BF16), aux_rows(total)], axis=0)


def fold(m, l, acc, received):
    other = join3(received[HD : HD + 3])
    peak = jnp.maximum(m, other)
    mine = jnp.exp2(m - peak)
    theirs = jnp.exp2(other - peak)
    return peak, l * mine + theirs, acc * mine + received[:HD].astype(F32) * theirs


def normal(m, l, acc):
    total = m + jnp.log2(l)
    return total, jnp.ones_like(total), acc / l


def merge_kernel(m, l, acc, rec, send_ref):
    send_ref[...] = pack(*fold(*normal(m[...], l[...], acc[...]), rec[:, ROWS:]))


def merge_cores(state, received):
    return pl.pallas_call(
        merge_kernel,
        out_shape=jax.ShapeDtypeStruct((HD + AUX, ROWS), BF16),
        compiler_params=params(),
        name="merge",
    )(*state, received)


def finish_kernel(m, l, acc, far, out_ref):
    _, total, summed = fold(m[...], l[...], acc[...], far[...])
    result = summed / total
    tokens, heads, _ = out_ref.shape
    for h in range(heads):
        out_ref[:, h, :] = result[:, h * tokens : (h + 1) * tokens].T.astype(BF16)


def finish(state, far, shape):
    return pl.pallas_call(
        finish_kernel,
        out_shape=jax.ShapeDtypeStruct(shape, BF16),
        compiler_params=params(),
        name="finish",
    )(*state, far)


def body(
    asker_vectors,
    asker_memory_pairs,
    leading_memory_pairs,
    document_memory_pairs,
    document_valid_extent,
    softening_factor,
):
    extent = document_valid_extent
    sending, q0 = prepared(extent, softening_factor, document_memory_pairs, asker_vectors)
    q1 = lax.ppermute(q0, "yh", shift(2, 1))
    q2 = lax.ppermute(q0, "c", shift(2, 1))
    moved = lax.all_to_all(sending, ("yl", "x"), 0, 0, tiled=True)
    cache = cache_block(after(asker_memory_pairs, q0), leading_memory_pairs)
    q3 = lax.ppermute(q1, "c", shift(2, 1))
    own = jnp.concatenate([moved.reshape(-1, HD), cache], axis=0)

    up, down = shift(RING, 1), shift(RING, -1)
    f1 = lax.ppermute(own, "z", up)
    b1 = lax.ppermute(own, "z", down)
    q0, q2, q1, q3 = lax.optimization_barrier((q0, q2, q1, q3))
    *state, queries = attend(extent, [q0, q2, q1, q3], None, [own], [(0, False)], "first")
    f2 = lax.ppermute(after(f1, state[0]), "z", up)
    b2 = lax.ppermute(after(b1, state[0]), "z", down)
    state = attend(extent, queries, state, [f1, b1], [(-1, False), (1, False)], "middle")
    f3 = lax.ppermute(after(f2, state[0]), "z", up)
    b3 = lax.ppermute(after(b2, state[0]), "z", down)
    state = attend(extent, queries, state, [f2, b2], [(-2, False), (2, False)], "middle")
    f4 = lax.ppermute(after(f3, state[0]), "z", up)
    cross = [(2 * z + c, 2 * ((z - 1) % RING) + 1 - c) for z in range(RING) for c in range(2)]
    b4 = lax.ppermute(after(b3, state[0]), ("z", "c"), cross)
    *state, packed = attend(extent, queries, state, [f3, b3], [(-3, False), (3, False)], "pack")
    received = lax.ppermute(after(packed, f4, b4), "c", shift(2, 1))
    rest = [(-4, False), (-4, True)]
    apart = attend(extent, queries, state, [f4, b4], rest, "part", None, 2 * ROWS)
    send = merge_cores(apart, received)
    far = lax.ppermute(send, "yh", shift(2, 1))
    kept = attend(extent, queries, state, [after(f4, send), b4], rest, "keep", received, 0)
    return finish(kept, far, asker_vectors.shape)


def solution(mesh):
    fine = Mesh(mesh.devices.reshape(8, 2, 2, 4, 2), ("z", "yh", "yl", "x", "c"))
    ctx, head = ("z", "yh"), ("yl", "x", "c")
    return jax.shard_map(
        body,
        mesh=fine,
        in_specs=(
            P(ctx, head, None),
            P(ctx, None, None),
            P(ctx, None, None),
            P(ctx + head, None, None),
            P(),
            P(head),
        ),
        out_specs=P(ctx, head, None),
        check_vma=False,
    )
```

```python
import functools
import math

import jax
import jax.numpy as jnp
from jax import lax
from jax.experimental import pallas as pl
from jax.experimental.pallas import tpu as pltpu
from jax.sharding import Mesh
from jax.sharding import PartitionSpec as P

F32 = jnp.float32
BF16 = jnp.bfloat16
KVH = 8
HD = 128
TILE = 256
RING = 8
SEND = 64
ROWS = 1024
BLOCKS = 4
AUX = 16
ASKED = 128
LED = 32
CACHE_ROWS = 2 * (ASKED + LED)
UNROLL = 2
SUB = 1024
MASKED = -1e30
LIMIT = 2.0**110
LOG2E = math.log2(math.e)
SCALE2 = LOG2E / math.sqrt(HD)
VMEM_LIMIT = 24 * 2**20


def shift(count, step):
    return [(i, (i + step) % count) for i in range(count)]


def params():
    return pltpu.CompilerParams(vmem_limit_bytes=VMEM_LIMIT)


def whole(shape):
    return pl.BlockSpec(shape, lambda *_: (0,) * len(shape))


def after(x, *others):
    return lax.optimization_barrier((x, *others))[0]


def split3(x):
    hi = x.astype(BF16)
    rest = x - hi.astype(F32)
    mid = rest.astype(BF16)
    low = (rest - mid.astype(F32)).astype(BF16)
    return hi, mid, low


def join3(rows):
    r = rows.astype(F32)
    return r[0:1] + r[1:2] + r[2:3]


def aux_rows(x):
    hi, mid, low = split3(x)
    pad = jnp.zeros((AUX - 3, x.shape[1]), F32)
    parts = [hi.astype(F32), mid.astype(F32), low.astype(F32), pad]
    return jnp.concatenate(parts, axis=0).astype(BF16)


def live_counts(extent_ref, zpos, cpos):
    base = (2 * zpos + lax.axis_index("yh")) * 4
    start = cpos * SEND
    return [extent_ref[base + j // 2] - (j % 2) * 128 - start for j in range(KVH)]


def prepare(extent_hbm, soft_hbm, doc_hbm, q_hbm, doc_out, q_out, extent_ref, soft_ref, doc_ref, q_ref, sems):
    pairs = ((extent_hbm, extent_ref), (doc_hbm, doc_ref), (soft_hbm, soft_ref), (q_hbm, q_ref))
    copies = [pltpu.make_async_copy(src, dst, sems.at[i]) for i, (src, dst) in enumerate(pairs)]
    for copy in copies:
        copy.start()
    copies[0].wait()
    copies[1].wait()
    rows = doc_ref.shape[0]
    own = lax.axis_index("yl") * 4 + lax.axis_index("x")
    live = jnp.int32(0)
    for j, count in enumerate(live_counts(extent_ref, lax.axis_index("z"), lax.axis_index("c"))):
        live = jnp.where(own == j, count, live)
    keep = lax.broadcasted_iota(jnp.int32, (rows, HD), 0) < live
    for g in range(KVH):
        for s in range(2):
            doc_out[g, s] = jnp.where(keep, doc_ref[:, 2 * g + s, :].astype(F32), 0.0).astype(BF16)
    copies[2].wait()
    copies[3].wait()
    tokens, heads, _ = q_ref.shape
    for h in range(heads):
        cols = slice(h * tokens, (h + 1) * tokens)
        q_out[:HD, cols] = q_ref[:, h, :].astype(F32).T.astype(BF16)
        factor = jnp.full((1, tokens), 1.0, F32) / soft_ref[h] * SCALE2
        q_out[HD:, cols] = aux_rows(factor)


def prepared(extent, softening_factor, document_memory_pairs, asker_vectors):
    rows = document_memory_pairs.shape[0]
    tokens, heads, _ = asker_vectors.shape
    vmem = pl.BlockSpec(memory_space=pltpu.VMEM)
    return pl.pallas_call(
        prepare,
        in_specs=[pl.BlockSpec(memory_space=pltpu.HBM)] * 4,
        out_specs=[vmem, vmem],
        out_shape=[
            jax.ShapeDtypeStruct((KVH, 2, rows, HD), BF16),
            jax.ShapeDtypeStruct((HD + AUX, tokens * heads), BF16),
        ],
        scratch_shapes=[
            pltpu.SMEM(extent.shape, jnp.int32),
            pltpu.SMEM(softening_factor.shape, F32),
            pltpu.VMEM(document_memory_pairs.shape, BF16),
            pltpu.VMEM(asker_vectors.shape, BF16),
            pltpu.SemaphoreType.DMA((4,)),
        ],
        compiler_params=params(),
        name="prepare",
    )(*[pltpu.with_memory_space_constraint(x, pltpu.HBM) for x in (extent, softening_factor, document_memory_pairs, asker_vectors)])


def prepare_caches(asker_ref, lead_ref, out_ref):
    own = lax.axis_index("yl") * 4 + lax.axis_index("x")
    c = lax.axis_index("c")
    half, lead = asker_ref.shape[0] // 2, lead_ref.shape[0] // 2
    mine = pl.ds(pl.multiple_of(c * half, half), half)
    led = pl.ds(pl.multiple_of(c * lead, lead), lead)
    for g in range(KVH):

        @pl.when(own == g)
        def _():
            for s in range(2):
                out_ref[s * half : (s + 1) * half, :] = asker_ref[mine, 2 * g + s, :]
                at = 2 * half + s * lead
                out_ref[at : at + lead, :] = lead_ref[led, 2 * g + s, :]


def cache_block(asker_memory_pairs, leading_memory_pairs):
    return pl.pallas_call(
        prepare_caches,
        out_shape=jax.ShapeDtypeStruct((CACHE_ROWS, HD), BF16),
        compiler_params=params(),
        name="caches",
    )(asker_memory_pairs, leading_memory_pairs)


def attend_kernel(shards, mode, q_low, *refs):
    refs = list(refs)
    extent_ref = refs.pop(0)
    first = mode == "first"
    count = len(shards)
    if first:
        parts = refs[:BLOCKS]
        pay = refs[BLOCKS : BLOCKS + count]
        m_out, l_out, acc_out, q_ref, k_ref, v_ref, m0, l0, acc0 = refs[BLOCKS + count :]
        for n, part in enumerate(parts):
            q_ref[:, n * ROWS : (n + 1) * ROWS] = part[...]
    else:
        q_ref, m0, l0, acc0 = refs[:4]
        pay = refs[4 : 4 + count]
        refs = refs[4 + count :]
        if mode in ("middle", "part"):
            m_out, l_out, acc_out, k_ref, v_ref = refs
        elif mode == "pack":
            m_out, l_out, acc_out, packed_ref, k_ref, v_ref = refs
        else:
            rec_ref, m_end, l_end, acc_end, k_ref, v_ref, m_out, l_out, acc_out = refs
    width = m_out.shape[1]
    zpos, ypos, cpos = lax.axis_index("z"), lax.axis_index("yh"), lax.axis_index("c")
    span = KVH * SEND
    asked_at = count * span
    led_at = asked_at + count * ASKED

    values, asked, led, alive, asked_alive = [], [], [], [], []
    for n, (ref, (away, swapped)) in enumerate(zip(pay, shards)):
        counts = live_counts(extent_ref, (zpos + away) % RING, 1 - cpos if swapped else cpos)
        lane = lax.broadcasted_iota(jnp.int32, (AUX, span), 1)
        bound = jnp.zeros((AUX, span), jnp.int32)
        for j in range(KVH):
            bound = jnp.where(lane // SEND == j, counts[j], bound)
            at = n * span + j * SEND
            k_ref[at : at + SEND, :] = ref[2 * j * SEND : (2 * j + 1) * SEND, :]
            values.append(ref[(2 * j + 1) * SEND : (2 * j + 2) * SEND, :])
        alive.append(jnp.where(lane % SEND < bound, 1.0, 0.0))
        at = 2 * span
        keys = ref[at : at + ASKED, :]
        vals = ref[at + ASKED : at + 2 * ASKED, :]
        if away == 0:
            asked_alive.append(jnp.ones((AUX, ASKED), F32))
        else:
            seen = (zpos + away >= 0) if away < 0 else (zpos + away >= RING)
            flag = jnp.where(seen, 1.0, 0.0).astype(F32)
            keys = (keys.astype(F32) * flag).astype(BF16)
            vals = (vals.astype(F32) * flag).astype(BF16)
            asked_alive.append(jnp.full((AUX, ASKED), 1.0, F32) * flag)
        k_ref[asked_at + n * ASKED : asked_at + (n + 1) * ASKED, :] = keys
        asked.append(vals)
        at += 2 * ASKED
        k_ref[led_at + n * LED : led_at + (n + 1) * LED, :] = ref[at : at + LED, :]
        led.append(ref[at + LED : at + 2 * LED, :])
    v_ref[:HD, :] = jnp.concatenate(values + asked + led, axis=0).T
    ones = [jnp.ones((AUX, count * LED), F32)]
    v_ref[HD:, :] = jnp.concatenate(alive + asked_alive + ones, axis=1).astype(BF16)

    if first:
        for i in range(width // SUB):
            cols = slice(i * SUB, (i + 1) * SUB)
            s = jnp.dot(k_ref[led_at:, :], q_ref[:HD, q_low + i * SUB : q_low + (i + 1) * SUB], preferred_element_type=F32) * SCALE2
            m0[:, cols] = jnp.max(s, axis=0, keepdims=True)
        l0[...] = jnp.zeros_like(l0)
        acc0[...] = jnp.zeros_like(acc0)

    def scores(start, size):
        cols = pl.ds(pl.multiple_of(start + q_low, 128), size)
        s = jnp.dot(k_ref[...], q_ref[:HD, cols], preferred_element_type=F32)
        factor = join3(q_ref[HD : HD + 3, cols])
        rest = s[asked_at:] * SCALE2
        if first:
            token = (lax.broadcasted_iota(jnp.int32, (1, size), 1) + start) % TILE
            yrow = jnp.where(start + q_low < 2 * ROWS, ypos, 1 - ypos)
            query = yrow * TILE + token
            key = ypos * TILE + cpos * ASKED + lax.broadcasted_iota(jnp.int32, (ASKED, 1), 0)
            near = jnp.where(key <= query, rest[:ASKED], MASKED)
            rest = jnp.concatenate([near, rest[ASKED:]], axis=0)
        return jnp.concatenate([s[:asked_at] * factor, rest], axis=0)

    def lazy(i, excess):
        start = pl.multiple_of(i * SUB, SUB)
        cols = pl.ds(start, SUB)
        old = pl.ds(pl.multiple_of(start + q_low, 128), SUB)
        s = scores(start, SUB)
        base = m0[:, old]
        p = jnp.exp2(s - base).astype(BF16)
        o = jnp.dot(v_ref[...], p, preferred_element_type=F32)
        m_out[:, cols] = base
        l_out[:, cols] = l0[:, old] + o[HD : HD + 1]
        acc_out[:, cols] = acc0[:, old] + o[:HD]
        return jnp.where(o[HD : HD + 1] <= LIMIT, excess, 1.0)

    excess = lax.fori_loop(0, width // SUB, lazy, jnp.zeros((1, SUB), F32), unroll=min(UNROLL, width // SUB))

    @pl.when(jnp.max(excess) > 0.5)
    def _():
        total = k_ref.shape[0]
        living = jnp.broadcast_to(v_ref[HD : HD + 1, :].astype(F32), (128, total)).T

        def exact(i, carry):
            start = pl.multiple_of(i * 128, 128)
            cols = pl.ds(start, 128)
            old = pl.ds(pl.multiple_of(start + q_low, 128), 128)
            s = jnp.where(living > 0.5, scores(start, 128), MASKED)
            base = m0[:, old]
            peak = jnp.maximum(base, jnp.max(s, axis=0, keepdims=True))
            shrink = jnp.exp2(base - peak)
            p = jnp.exp2(s - peak).astype(BF16)
            o = jnp.dot(v_ref[...], p, preferred_element_type=F32)
            m_out[:, cols] = peak
            l_out[:, cols] = l0[:, old] * shrink + o[HD : HD + 1]
            acc_out[:, cols] = acc0[:, old] * shrink + o[:HD]
            return carry

        lax.fori_loop(0, width // 128, exact, 0)

    if mode == "pack":
        for n in range(2):
            cols = slice((2 * n + 1) * ROWS, (2 * n + 2) * ROWS)
            packed_ref[:, n * ROWS : (n + 1) * ROWS] = pack(m_out[:, cols], l_out[:, cols], acc_out[:, cols])
    if mode == "keep":
        m_end[...], l_end[...], acc_end[...] = fold(*normal(m_out[...], l_out[...], acc_out[...]), rec_ref[:, :ROWS])


def state_shapes(width):
    return [
        jax.ShapeDtypeStruct((1, width), F32),
        jax.ShapeDtypeStruct((1, width), F32),
        jax.ShapeDtypeStruct((HD, width), F32),
    ]


def attend(extent, queries, state, pays, shards, mode, received=None, q_low=0):
    keys = len(shards) * (KVH * SEND + ASKED + LED)
    width = ROWS if mode in ("part", "keep") else BLOCKS * ROWS
    scratch = [pltpu.VMEM((keys, HD), BF16), pltpu.VMEM((HD + AUX, keys), BF16)]
    floats = [pltpu.VMEM((1, width), F32), pltpu.VMEM((1, width), F32), pltpu.VMEM((HD, width), F32)]
    shapes = state_shapes(width)
    if mode == "first":
        args = [extent, *queries, *pays]
        shapes.append(jax.ShapeDtypeStruct((HD + AUX, width), BF16))
        scratch += floats
    else:
        args = [extent, queries, *state, *pays]
    if mode == "pack":
        shapes.append(jax.ShapeDtypeStruct((HD + AUX, 2 * ROWS), BF16))
    if mode == "keep":
        args.append(received)
        scratch += floats
    vmem = pl.BlockSpec(memory_space=pltpu.VMEM)
    return pl.pallas_call(
        functools.partial(attend_kernel, shards, mode, q_low),
        in_specs=[pl.BlockSpec(memory_space=pltpu.SMEM)] + [vmem] * (len(args) - 1),
        out_specs=[vmem] * len(shapes),
        out_shape=shapes,
        scratch_shapes=scratch,
        compiler_params=params(),
        name="attend",
    )(*args)


def pack(m, l, acc):
    total = m + jnp.log2(l)
    return jnp.concatenate([(acc / l).astype(BF16), aux_rows(total)], axis=0)


def fold(m, l, acc, received):
    other = join3(received[HD : HD + 3])
    peak = jnp.maximum(m, other)
    mine = jnp.exp2(m - peak)
    theirs = jnp.exp2(other - peak)
    return peak, l * mine + theirs, acc * mine + received[:HD].astype(F32) * theirs


def normal(m, l, acc):
    total = m + jnp.log2(l)
    return total, jnp.ones_like(total), acc / l


def merge_kernel(m, l, acc, rec, send_ref):
    send_ref[...] = pack(*fold(*normal(m[...], l[...], acc[...]), rec[:, ROWS:]))


def merge_cores(state, received):
    return pl.pallas_call(
        merge_kernel,
        out_shape=jax.ShapeDtypeStruct((HD + AUX, ROWS), BF16),
        compiler_params=params(),
        name="merge",
    )(*state, received)


def finish_kernel(m, l, acc, far, out_ref):
    _, total, summed = fold(m[...], l[...], acc[...], far[...])
    result = summed / total
    tokens, heads, _ = out_ref.shape
    for h in range(heads):
        out_ref[:, h, :] = result[:, h * tokens : (h + 1) * tokens].T.astype(BF16)


def finish(state, far, shape):
    return pl.pallas_call(
        finish_kernel,
        out_shape=jax.ShapeDtypeStruct(shape, BF16),
        compiler_params=params(),
        name="finish",
    )(*state, far)


def body(
    asker_vectors,
    asker_memory_pairs,
    leading_memory_pairs,
    document_memory_pairs,
    document_valid_extent,
    softening_factor,
):
    extent = document_valid_extent
    sending, q0 = prepared(extent, softening_factor, document_memory_pairs, asker_vectors)
    q1 = lax.ppermute(q0, "yh", shift(2, 1))
    q2 = lax.ppermute(q0, "c", shift(2, 1))
    moved = lax.all_to_all(sending, ("yl", "x"), 0, 0, tiled=True)
    cache = cache_block(after(asker_memory_pairs, q0), leading_memory_pairs)
    q3 = lax.ppermute(q1, "c", shift(2, 1))
    own = jnp.concatenate([after(moved, q1, q2).reshape(-1, HD), cache], axis=0)

    up, down = shift(RING, 1), shift(RING, -1)
    f1 = lax.ppermute(own, "z", up)
    b1 = lax.ppermute(own, "z", down)
    q0, q2, q1, q3 = lax.optimization_barrier((q0, q2, q1, q3))
    *state, queries = attend(extent, [q0, q2, q1, q3], None, [own], [(0, False)], "first")
    f2 = lax.ppermute(after(f1, state[0]), "z", up)
    b2 = lax.ppermute(after(b1, state[0]), "z", down)
    state = attend(extent, queries, state, [f1, b1], [(-1, False), (1, False)], "middle")
    f3 = lax.ppermute(after(f2, state[0]), "z", up)
    b3 = lax.ppermute(after(b2, state[0]), "z", down)
    state = attend(extent, queries, state, [f2, b2], [(-2, False), (2, False)], "middle")
    f4 = lax.ppermute(after(f3, state[0]), "z", up)
    cross = [(2 * z + c, 2 * ((z - 1) % RING) + 1 - c) for z in range(RING) for c in range(2)]
    b4 = lax.ppermute(after(b3, state[0]), ("z", "c"), cross)
    *state, packed = attend(extent, queries, state, [f3, b3], [(-3, False), (3, False)], "pack")
    received = lax.ppermute(after(packed, f4, b4), "c", shift(2, 1))
    rest = [(-4, False), (-4, True)]
    apart = attend(extent, queries, state, [f4, b4], rest, "part", None, 2 * ROWS)
    send = merge_cores(apart, received)
    far = lax.ppermute(send, "yh", shift(2, 1))
    kept = attend(extent, queries, state, [after(f4, send), b4], rest, "keep", received, 0)
    return finish(kept, far, asker_vectors.shape)


def solution(mesh):
    fine = Mesh(mesh.devices.reshape(8, 2, 2, 4, 2), ("z", "yh", "yl", "x", "c"))
    ctx, head = ("z", "yh"), ("yl", "x", "c")
    return jax.shard_map(
        body,
        mesh=fine,
        in_specs=(
            P(ctx, head, None),
            P(ctx, None, None),
            P(ctx, None, None),
            P(ctx + head, None, None),
            P(),
            P(head),
        ),
        out_specs=P(ctx, head, None),
        check_vma=False,
    )
```

```python
import functools
import math

import jax
import jax.numpy as jnp
from jax import lax
from jax.experimental import pallas as pl
from jax.experimental.pallas import tpu as pltpu
from jax.sharding import Mesh
from jax.sharding import PartitionSpec as P

F32 = jnp.float32
BF16 = jnp.bfloat16
KVH = 8
HD = 128
TILE = 256
RING = 8
SEND = 64
ROWS = 1024
BLOCKS = 4
AUX = 16
ASKED = 128
LED = 32
CACHE_ROWS = 2 * (ASKED + LED)
UNROLL = 2
SUB = 1024
MASKED = -1e30
LIMIT = 2.0**110
LOG2E = math.log2(math.e)
SCALE2 = LOG2E / math.sqrt(HD)
VMEM_LIMIT = 24 * 2**20


def shift(count, step):
    return [(i, (i + step) % count) for i in range(count)]


def params():
    return pltpu.CompilerParams(vmem_limit_bytes=VMEM_LIMIT)


def whole(shape):
    return pl.BlockSpec(shape, lambda *_: (0,) * len(shape))


def after(x, *others):
    return lax.optimization_barrier((x, *others))[0]


def split3(x):
    hi = x.astype(BF16)
    rest = x - hi.astype(F32)
    mid = rest.astype(BF16)
    low = (rest - mid.astype(F32)).astype(BF16)
    return hi, mid, low


def join3(rows):
    r = rows.astype(F32)
    return r[0:1] + r[1:2] + r[2:3]


def aux_rows(x):
    hi, mid, low = split3(x)
    pad = jnp.zeros((AUX - 3, x.shape[1]), F32)
    parts = [hi.astype(F32), mid.astype(F32), low.astype(F32), pad]
    return jnp.concatenate(parts, axis=0).astype(BF16)


def live_counts(extent_ref, zpos, ypos, cpos):
    base = (2 * zpos + ypos) * 4
    start = cpos * SEND
    return [extent_ref[base + j // 2] - (j % 2) * 128 - start for j in range(KVH)]


def prepare(extent_hbm, soft_hbm, doc_hbm, q_hbm, doc_out, q_out, extent_ref, soft_ref, doc_ref, q_ref, sems):
    pairs = ((extent_hbm, extent_ref), (doc_hbm, doc_ref), (soft_hbm, soft_ref), (q_hbm, q_ref))
    copies = [pltpu.make_async_copy(src, dst, sems.at[i]) for i, (src, dst) in enumerate(pairs)]
    for copy in copies:
        copy.start()
    copies[0].wait()
    copies[1].wait()
    rows = doc_ref.shape[0]
    own = lax.axis_index("yl") * 4 + lax.axis_index("x")
    live = jnp.int32(0)
    for j, count in enumerate(live_counts(extent_ref, lax.axis_index("z"), lax.axis_index("yh"), lax.axis_index("c"))):
        live = jnp.where(own == j, count, live)
    keep = lax.broadcasted_iota(jnp.int32, (rows, HD), 0) < live
    for g in range(KVH):
        for s in range(2):
            doc_out[g, s] = jnp.where(keep, doc_ref[:, 2 * g + s, :].astype(F32), 0.0).astype(BF16)
    copies[2].wait()
    copies[3].wait()
    tokens, heads, _ = q_ref.shape
    for h in range(heads):
        cols = slice(h * tokens, (h + 1) * tokens)
        q_out[:HD, cols] = q_ref[:, h, :].astype(F32).T.astype(BF16)
        factor = jnp.full((1, tokens), 1.0, F32) / soft_ref[h] * SCALE2
        q_out[HD:, cols] = aux_rows(factor)


def prepared(extent, softening_factor, document_memory_pairs, asker_vectors):
    rows = document_memory_pairs.shape[0]
    tokens, heads, _ = asker_vectors.shape
    vmem = pl.BlockSpec(memory_space=pltpu.VMEM)
    return pl.pallas_call(
        prepare,
        in_specs=[pl.BlockSpec(memory_space=pltpu.HBM)] * 4,
        out_specs=[vmem, vmem],
        out_shape=[
            jax.ShapeDtypeStruct((KVH, 2, rows, HD), BF16),
            jax.ShapeDtypeStruct((HD + AUX, tokens * heads), BF16),
        ],
        scratch_shapes=[
            pltpu.SMEM(extent.shape, jnp.int32),
            pltpu.SMEM(softening_factor.shape, F32),
            pltpu.VMEM(document_memory_pairs.shape, BF16),
            pltpu.VMEM(asker_vectors.shape, BF16),
            pltpu.SemaphoreType.DMA((4,)),
        ],
        compiler_params=params(),
        name="prepare",
    )(*[pltpu.with_memory_space_constraint(x, pltpu.HBM) for x in (extent, softening_factor, document_memory_pairs, asker_vectors)])


def prepare_caches(asker_ref, lead_ref, out_ref):
    own = lax.axis_index("yl") * 4 + lax.axis_index("x")
    c = lax.axis_index("c")
    half, lead = asker_ref.shape[0] // 2, lead_ref.shape[0] // 2
    mine = pl.ds(pl.multiple_of(c * half, half), half)
    led = pl.ds(pl.multiple_of(c * lead, lead), lead)
    for g in range(KVH):

        @pl.when(own == g)
        def _():
            for s in range(2):
                out_ref[s * half : (s + 1) * half, :] = asker_ref[mine, 2 * g + s, :]
                at = 2 * half + s * lead
                out_ref[at : at + lead, :] = lead_ref[led, 2 * g + s, :]


def cache_block(asker_memory_pairs, leading_memory_pairs):
    return pl.pallas_call(
        prepare_caches,
        out_shape=jax.ShapeDtypeStruct((CACHE_ROWS, HD), BF16),
        compiler_params=params(),
        name="caches",
    )(asker_memory_pairs, leading_memory_pairs)


def attend_kernel(shards, mode, q_low, *refs):
    refs = list(refs)
    extent_ref = refs.pop(0)
    first = mode == "first"
    count = len(shards)
    if first:
        parts = refs[:BLOCKS]
        pay = refs[BLOCKS : BLOCKS + count]
        m_out, l_out, acc_out, q_ref, k_ref, v_ref, m0, l0, acc0 = refs[BLOCKS + count :]
        for n, part in enumerate(parts):
            q_ref[:, n * ROWS : (n + 1) * ROWS] = part[...]
    else:
        q_ref, m0, l0, acc0 = refs[:4]
        pay = refs[4 : 4 + count]
        refs = refs[4 + count :]
        if mode == "pack":
            m_out, l_out, acc_out, packed_ref, k_ref, v_ref = refs
        elif mode == "only":
            packed_ref, k_ref, v_ref, m_out, l_out, acc_out = refs
        else:
            m_out, l_out, acc_out, k_ref, v_ref = refs
    width = m_out.shape[1]
    zpos, ypos, cpos = lax.axis_index("z"), lax.axis_index("yh"), lax.axis_index("c")
    span = KVH * SEND
    asked_at = count * span
    led_at = asked_at + count * ASKED

    values, asked, led, alive, asked_alive = [], [], [], [], []
    for n, (ref, (away, swapped)) in enumerate(zip(pay, shards)):
        counts = live_counts(extent_ref, (zpos + away) % RING, 1 - ypos if swapped else ypos, cpos)
        lane = lax.broadcasted_iota(jnp.int32, (AUX, span), 1)
        bound = jnp.zeros((AUX, span), jnp.int32)
        for j in range(KVH):
            bound = jnp.where(lane // SEND == j, counts[j], bound)
            at = n * span + j * SEND
            k_ref[at : at + SEND, :] = ref[2 * j * SEND : (2 * j + 1) * SEND, :]
            values.append(ref[(2 * j + 1) * SEND : (2 * j + 2) * SEND, :])
        alive.append(jnp.where(lane % SEND < bound, 1.0, 0.0))
        at = 2 * span
        keys = ref[at : at + ASKED, :]
        vals = ref[at + ASKED : at + 2 * ASKED, :]
        if away == 0:
            asked_alive.append(jnp.ones((AUX, ASKED), F32))
        else:
            seen = (zpos + away >= 0) if away < 0 else (zpos + away >= RING)
            flag = jnp.where(seen, 1.0, 0.0).astype(F32)
            keys = (keys.astype(F32) * flag).astype(BF16)
            vals = (vals.astype(F32) * flag).astype(BF16)
            asked_alive.append(jnp.full((AUX, ASKED), 1.0, F32) * flag)
        k_ref[asked_at + n * ASKED : asked_at + (n + 1) * ASKED, :] = keys
        asked.append(vals)
        at += 2 * ASKED
        k_ref[led_at + n * LED : led_at + (n + 1) * LED, :] = ref[at : at + LED, :]
        led.append(ref[at + LED : at + 2 * LED, :])
    v_ref[:HD, :] = jnp.concatenate(values + asked + led, axis=0).T
    ones = [jnp.ones((AUX, count * LED), F32)]
    v_ref[HD:, :] = jnp.concatenate(alive + asked_alive + ones, axis=1).astype(BF16)

    if first:
        for i in range(width // SUB):
            cols = slice(i * SUB, (i + 1) * SUB)
            s = jnp.dot(k_ref[led_at:, :], q_ref[:HD, q_low + i * SUB : q_low + (i + 1) * SUB], preferred_element_type=F32) * SCALE2
            m0[:, cols] = jnp.max(s, axis=0, keepdims=True)
        l0[...] = jnp.zeros_like(l0)
        acc0[...] = jnp.zeros_like(acc0)

    def scores(start, size):
        cols = pl.ds(pl.multiple_of(start + q_low, 128), size)
        s = jnp.dot(k_ref[...], q_ref[:HD, cols], preferred_element_type=F32)
        factor = join3(q_ref[HD:, cols])
        rest = s[asked_at:] * SCALE2
        if first:
            token = (lax.broadcasted_iota(jnp.int32, (1, size), 1) + start) % TILE
            yrow = jnp.where(start + q_low < 2 * ROWS, ypos, 1 - ypos)
            query = yrow * TILE + token
            key = ypos * TILE + cpos * ASKED + lax.broadcasted_iota(jnp.int32, (ASKED, 1), 0)
            near = jnp.where(key <= query, rest[:ASKED], MASKED)
            rest = jnp.concatenate([near, rest[ASKED:]], axis=0)
        return jnp.concatenate([s[:asked_at] * factor, rest], axis=0)

    def lazy(i, excess):
        start = pl.multiple_of(i * SUB, SUB)
        cols = pl.ds(start, SUB)
        old = pl.ds(pl.multiple_of(start + q_low, 128), SUB)
        s = scores(start, SUB)
        base = m0[:, old]
        p = jnp.exp2(s - base).astype(BF16)
        o = jnp.dot(v_ref[...], p, preferred_element_type=F32)
        m_out[:, cols] = base
        l_out[:, cols] = l0[:, old] + o[HD : HD + 1]
        acc_out[:, cols] = acc0[:, old] + o[:HD]
        return jnp.where(o[HD : HD + 1] <= LIMIT, excess, 1.0)

    excess = lax.fori_loop(0, width // SUB, lazy, jnp.zeros((1, SUB), F32), unroll=min(UNROLL, width // SUB))

    @pl.when(jnp.max(excess) > 0.5)
    def _():
        total = k_ref.shape[0]
        living = jnp.broadcast_to(v_ref[HD:, :].astype(F32)[:1], (128, total)).T

        def exact(i, carry):
            start = pl.multiple_of(i * 128, 128)
            cols = pl.ds(start, 128)
            old = pl.ds(pl.multiple_of(start + q_low, 128), 128)
            s = jnp.where(living > 0.5, scores(start, 128), MASKED)
            base = m0[:, old]
            peak = jnp.maximum(base, jnp.max(s, axis=0, keepdims=True))
            shrink = jnp.exp2(base - peak)
            p = jnp.exp2(s - peak).astype(BF16)
            o = jnp.dot(v_ref[...], p, preferred_element_type=F32)
            m_out[:, cols] = peak
            l_out[:, cols] = l0[:, old] * shrink + o[HD : HD + 1]
            acc_out[:, cols] = acc0[:, old] * shrink + o[:HD]
            return carry

        lax.fori_loop(0, width // 128, exact, 0)

    if mode in ("pack", "only"):
        cols = slice(width - ROWS, width)
        packed_ref[...] = pack(m_out[:, cols], l_out[:, cols], acc_out[:, cols])


def state_shapes(width):
    return [
        jax.ShapeDtypeStruct((1, width), F32),
        jax.ShapeDtypeStruct((1, width), F32),
        jax.ShapeDtypeStruct((HD, width), F32),
    ]


def attend(extent, queries, state, pays, shards, mode, q_low=0, width=BLOCKS * ROWS):
    keys = len(shards) * (KVH * SEND + ASKED + LED)
    scratch = [pltpu.VMEM((keys, HD), BF16), pltpu.VMEM((HD + AUX, keys), BF16)]
    shapes = state_shapes(width)
    if mode == "first":
        args = [extent, *queries, *pays]
        shapes.append(jax.ShapeDtypeStruct((HD + AUX, width), BF16))
        scratch += [pltpu.VMEM((1, width), F32), pltpu.VMEM((1, width), F32), pltpu.VMEM((HD, width), F32)]
    else:
        args = [extent, queries, *state, *pays]
    if mode == "only":
        shapes = []
        scratch += [pltpu.VMEM((1, width), F32), pltpu.VMEM((1, width), F32), pltpu.VMEM((HD, width), F32)]
    if mode in ("pack", "only"):
        shapes.append(jax.ShapeDtypeStruct((HD + AUX, ROWS), BF16))
    vmem = pl.BlockSpec(memory_space=pltpu.VMEM)
    return pl.pallas_call(
        functools.partial(attend_kernel, shards, mode, q_low),
        in_specs=[pl.BlockSpec(memory_space=pltpu.SMEM)] + [vmem] * (len(args) - 1),
        out_specs=[vmem] * len(shapes),
        out_shape=shapes,
        scratch_shapes=scratch,
        compiler_params=params(),
        name="attend",
    )(*args)


def pack(m, l, acc):
    total = m + jnp.log2(l)
    return jnp.concatenate([(acc * (1.0 / l)).astype(BF16), aux_rows(total)], axis=0)


def fold(m, l, acc, received):
    other = join3(received[HD : HD + 3])
    peak = jnp.maximum(m, other)
    mine = jnp.exp2(m - peak)
    theirs = jnp.exp2(other - peak)
    return peak, l * mine + theirs, acc * mine + received[:HD].astype(F32) * theirs


def normal(m, l, acc):
    total = m + jnp.log2(l)
    return total, jnp.ones_like(total), acc * (1.0 / l)


def merge_kernel(m, l, acc, rec, send_ref):
    send_ref[...] = pack(*fold(*normal(m[:, :ROWS], l[:, :ROWS], acc[:, :ROWS]), rec[...]))


def merge_cores(state, received):
    return pl.pallas_call(
        merge_kernel,
        out_shape=jax.ShapeDtypeStruct((HD + AUX, ROWS), BF16),
        compiler_params=params(),
        name="merge",
    )(*state, received)


def finish_kernel(m, l, acc, rec, far, out_ref):
    near = fold(*normal(m[...], l[...], acc[...]), rec[...])
    _, total, summed = fold(*near, far[...])
    result = (summed * (1.0 / total)).astype(BF16)
    tokens, heads, _ = out_ref.shape
    parts = [result[:, h * tokens : (h + 1) * tokens].T for h in range(heads)]
    out_ref[...] = jnp.stack(parts, axis=1)


def finish(state, received, far, shape):
    return pl.pallas_call(
        finish_kernel,
        out_shape=jax.ShapeDtypeStruct(shape, BF16),
        compiler_params=params(),
        name="finish",
    )(*state, received, far)


def body(
    asker_vectors,
    asker_memory_pairs,
    leading_memory_pairs,
    document_memory_pairs,
    document_valid_extent,
    softening_factor,
):
    extent = document_valid_extent
    sending, q0 = prepared(extent, softening_factor, document_memory_pairs, asker_vectors)
    q1 = lax.ppermute(q0, "yh", shift(2, 1))
    q2 = lax.ppermute(q0, "c", shift(2, 1))
    moved = lax.all_to_all(sending, ("yl", "x"), 0, 0, tiled=True)
    cache = cache_block(after(asker_memory_pairs, q0), leading_memory_pairs)
    q3 = lax.ppermute(q1, "c", shift(2, 1))
    own = jnp.concatenate([after(moved, q1, q2).reshape(-1, HD), cache], axis=0)

    up, down = shift(RING, 1), shift(RING, -1)
    f1 = lax.ppermute(own, "z", up)
    b1 = lax.ppermute(own, "z", down)
    q0, q2, q1, q3 = lax.optimization_barrier((q0, q2, q1, q3))
    *state, queries = attend(extent, [q0, q2, q1, q3], None, [own], [(0, False)], "first")
    f2 = lax.ppermute(after(f1, state[0]), "z", up)
    b2 = lax.ppermute(after(b1, state[0]), "z", down)
    state = attend(extent, queries, state, [f1, b1], [(-1, False), (1, False)], "middle")
    f3 = lax.ppermute(after(f2, state[0]), "z", up)
    b3 = lax.ppermute(after(b2, state[0]), "z", down)
    state = attend(extent, queries, state, [f2, b2], [(-2, False), (2, False)], "middle")
    f4 = lax.ppermute(after(f3, state[0]), "z", up)
    cross = [(2 * z + y, 2 * ((z - 1) % RING) + 1 - y) for z in range(RING) for y in range(2)]
    b4 = lax.ppermute(after(b3, state[0]), ("z", "yh"), cross)
    half = 2 * ROWS
    last = [(-3, False), (3, False)]
    *apart, packed = attend(extent, queries, state, [f3, b3], last, "pack", half, half)
    received = lax.ppermute(packed, "c", shift(2, 1))
    send = merge_cores(apart, received)
    far = lax.ppermute(send, "yh", shift(2, 1))
    state = attend(extent, queries, state, [after(f3, send), b3], last, "middle", 0, half)
    rest = [(-4, False), (-4, True)]
    (packed,) = attend(extent, queries, state, [f4, b4], rest, "only", ROWS, ROWS)
    received = lax.ppermute(packed, "c", shift(2, 1))
    kept = attend(extent, queries, state, [after(f4, packed), b4], rest, "middle", 0, ROWS)
    return finish(kept, received, far, asker_vectors.shape)


def solution(mesh):
    fine = Mesh(mesh.devices.reshape(8, 2, 2, 4, 2), ("z", "yh", "yl", "x", "c"))
    ctx, head = ("z", "yh"), ("yl", "x", "c")
    return jax.shard_map(
        body,
        mesh=fine,
        in_specs=(
            P(ctx, head, None),
            P(ctx, None, None),
            P(ctx, None, None),
            P(ctx + head, None, None),
            P(),
            P(head),
        ),
        out_specs=P(ctx, head, None),
        check_vma=False,
    )
```

```python
import functools
import math

import jax
import jax.numpy as jnp
from jax import lax
from jax.experimental import pallas as pl
from jax.experimental.pallas import tpu as pltpu
from jax.sharding import Mesh
from jax.sharding import PartitionSpec as P

F32 = jnp.float32
BF16 = jnp.bfloat16
KVH = 8
HD = 128
TILE = 256
RING = 8
SEND = 64
ROWS = 1024
BLOCKS = 4
AUX = 16
ASKED = 128
LED = 32
CACHE_ROWS = 2 * (ASKED + LED)
UNROLL = 2
SUB = 1024
MASKED = -1e30
LIMIT = 2.0**110
LOG2E = math.log2(math.e)
SCALE2 = LOG2E / math.sqrt(HD)
VMEM_LIMIT = 24 * 2**20


def shift(count, step):
    return [(i, (i + step) % count) for i in range(count)]


def params():
    return pltpu.CompilerParams(vmem_limit_bytes=VMEM_LIMIT)


def whole(shape):
    return pl.BlockSpec(shape, lambda *_: (0,) * len(shape))


def after(x, *others):
    return lax.optimization_barrier((x, *others))[0]


def split3(x):
    hi = x.astype(BF16)
    rest = x - hi.astype(F32)
    mid = rest.astype(BF16)
    low = (rest - mid.astype(F32)).astype(BF16)
    return hi, mid, low


def join3(rows):
    r = rows.astype(F32)
    return r[0:1] + r[1:2] + r[2:3]


def aux_rows(x):
    hi, mid, low = split3(x)
    pad = jnp.zeros((AUX - 3, x.shape[1]), F32)
    parts = [hi.astype(F32), mid.astype(F32), low.astype(F32), pad]
    return jnp.concatenate(parts, axis=0).astype(BF16)


def live_counts(extent_ref, zpos, ypos, cpos):
    base = (2 * zpos + ypos) * 4
    start = cpos * SEND
    return [extent_ref[base + j // 2] - (j % 2) * 128 - start for j in range(KVH)]


def prepare(extent_hbm, soft_hbm, doc_hbm, q_hbm, doc_out, q_out, bare_out, extent_ref, soft_ref, doc_ref, q_ref, sems):
    pairs = ((extent_hbm, extent_ref), (doc_hbm, doc_ref), (soft_hbm, soft_ref), (q_hbm, q_ref))
    copies = [pltpu.make_async_copy(src, dst, sems.at[i]) for i, (src, dst) in enumerate(pairs)]
    for copy in copies:
        copy.start()
    copies[0].wait()
    copies[1].wait()
    rows = doc_ref.shape[0]
    own = lax.axis_index("yl") * 4 + lax.axis_index("x")
    live = jnp.int32(0)
    for j, count in enumerate(live_counts(extent_ref, lax.axis_index("z"), lax.axis_index("yh"), lax.axis_index("c"))):
        live = jnp.where(own == j, count, live)
    keep = lax.broadcasted_iota(jnp.int32, (rows, HD), 0) < live
    for g in range(KVH):
        for s in range(2):
            doc_out[g, s] = jnp.where(keep, doc_ref[:, 2 * g + s, :].astype(F32), 0.0).astype(BF16)
    copies[2].wait()
    copies[3].wait()
    tokens, heads, _ = q_ref.shape
    for h in range(heads):
        cols = slice(h * tokens, (h + 1) * tokens)
        turned = q_ref[:, h, :].astype(F32).T.astype(BF16)
        q_out[:HD, cols] = turned
        bare_out[:, cols] = turned
        factor = jnp.full((1, tokens), 1.0, F32) / soft_ref[h] * SCALE2
        q_out[HD:, cols] = aux_rows(factor)


def prepared(extent, softening_factor, document_memory_pairs, asker_vectors):
    rows = document_memory_pairs.shape[0]
    tokens, heads, _ = asker_vectors.shape
    vmem = pl.BlockSpec(memory_space=pltpu.VMEM)
    return pl.pallas_call(
        prepare,
        in_specs=[pl.BlockSpec(memory_space=pltpu.HBM)] * 4,
        out_specs=[vmem, vmem, vmem],
        out_shape=[
            jax.ShapeDtypeStruct((KVH, 2, rows, HD), BF16),
            jax.ShapeDtypeStruct((HD + AUX, tokens * heads), BF16),
            jax.ShapeDtypeStruct((HD, tokens * heads), BF16),
        ],
        scratch_shapes=[
            pltpu.SMEM(extent.shape, jnp.int32),
            pltpu.SMEM(softening_factor.shape, F32),
            pltpu.VMEM(document_memory_pairs.shape, BF16),
            pltpu.VMEM(asker_vectors.shape, BF16),
            pltpu.SemaphoreType.DMA((4,)),
        ],
        compiler_params=params(),
        name="prepare",
    )(*[pltpu.with_memory_space_constraint(x, pltpu.HBM) for x in (extent, softening_factor, document_memory_pairs, asker_vectors)])


def prepare_caches(asker_ref, lead_ref, out_ref):
    own = lax.axis_index("yl") * 4 + lax.axis_index("x")
    c = lax.axis_index("c")
    half, lead = asker_ref.shape[0] // 2, lead_ref.shape[0] // 2
    mine = pl.ds(pl.multiple_of(c * half, half), half)
    led = pl.ds(pl.multiple_of(c * lead, lead), lead)
    for g in range(KVH):

        @pl.when(own == g)
        def _():
            for s in range(2):
                out_ref[s * half : (s + 1) * half, :] = asker_ref[mine, 2 * g + s, :]
                at = 2 * half + s * lead
                out_ref[at : at + lead, :] = lead_ref[led, 2 * g + s, :]


def cache_block(asker_memory_pairs, leading_memory_pairs):
    return pl.pallas_call(
        prepare_caches,
        out_shape=jax.ShapeDtypeStruct((CACHE_ROWS, HD), BF16),
        compiler_params=params(),
        name="caches",
    )(asker_memory_pairs, leading_memory_pairs)


def attend_kernel(shards, mode, q_low, *refs):
    refs = list(refs)
    extent_ref = refs.pop(0)
    first = mode == "first"
    count = len(shards)
    if first:
        parts = refs[:BLOCKS]
        pay = refs[BLOCKS : BLOCKS + count]
        m_out, l_out, acc_out, q_ref, k_ref, v_ref, m0, l0, acc0 = refs[BLOCKS + count :]
        for n, part in enumerate(parts):
            q_ref[:HD, n * ROWS : (n + 1) * ROWS] = part[:HD, :]
            q_ref[HD:, n * ROWS : (n + 1) * ROWS] = parts[n % 2][HD:, :]
    else:
        q_ref, m0, l0, acc0 = refs[:4]
        pay = refs[4 : 4 + count]
        refs = refs[4 + count :]
        if mode == "pack":
            m_out, l_out, acc_out, packed_ref, k_ref, v_ref = refs
        elif mode == "only":
            packed_ref, k_ref, v_ref, m_out, l_out, acc_out = refs
        else:
            m_out, l_out, acc_out, k_ref, v_ref = refs
    width = m_out.shape[1]
    zpos, ypos, cpos = lax.axis_index("z"), lax.axis_index("yh"), lax.axis_index("c")
    span = KVH * SEND
    asked_at = count * span
    led_at = asked_at + count * ASKED

    values, asked, led, alive, asked_alive = [], [], [], [], []
    for n, (ref, (away, swapped)) in enumerate(zip(pay, shards)):
        counts = live_counts(extent_ref, (zpos + away) % RING, 1 - ypos if swapped else ypos, cpos)
        lane = lax.broadcasted_iota(jnp.int32, (AUX, span), 1)
        bound = jnp.zeros((AUX, span), jnp.int32)
        for j in range(KVH):
            bound = jnp.where(lane // SEND == j, counts[j], bound)
            at = n * span + j * SEND
            k_ref[at : at + SEND, :] = ref[2 * j * SEND : (2 * j + 1) * SEND, :]
            values.append(ref[(2 * j + 1) * SEND : (2 * j + 2) * SEND, :])
        alive.append(jnp.where(lane % SEND < bound, 1.0, 0.0))
        at = 2 * span
        keys = ref[at : at + ASKED, :]
        vals = ref[at + ASKED : at + 2 * ASKED, :]
        if away == 0:
            asked_alive.append(jnp.ones((AUX, ASKED), F32))
        else:
            seen = (zpos + away >= 0) if away < 0 else (zpos + away >= RING)
            flag = jnp.where(seen, 1.0, 0.0).astype(F32)
            keys = (keys.astype(F32) * flag).astype(BF16)
            vals = (vals.astype(F32) * flag).astype(BF16)
            asked_alive.append(jnp.full((AUX, ASKED), 1.0, F32) * flag)
        k_ref[asked_at + n * ASKED : asked_at + (n + 1) * ASKED, :] = keys
        asked.append(vals)
        at += 2 * ASKED
        k_ref[led_at + n * LED : led_at + (n + 1) * LED, :] = ref[at : at + LED, :]
        led.append(ref[at + LED : at + 2 * LED, :])
    v_ref[:HD, :] = jnp.concatenate(values + asked + led, axis=0).T
    ones = [jnp.ones((AUX, count * LED), F32)]
    v_ref[HD:, :] = jnp.concatenate(alive + asked_alive + ones, axis=1).astype(BF16)

    if first:
        for i in range(width // SUB):
            cols = slice(i * SUB, (i + 1) * SUB)
            s = jnp.dot(k_ref[led_at:, :], q_ref[:HD, q_low + i * SUB : q_low + (i + 1) * SUB], preferred_element_type=F32) * SCALE2
            m0[:, cols] = jnp.max(s, axis=0, keepdims=True)
        l0[...] = jnp.zeros_like(l0)
        acc0[...] = jnp.zeros_like(acc0)

    def scores(start, size):
        cols = pl.ds(pl.multiple_of(start + q_low, 128), size)
        s = jnp.dot(k_ref[...], q_ref[:HD, cols], preferred_element_type=F32)
        factor = join3(q_ref[HD:, cols])
        rest = s[asked_at:] * SCALE2
        if first:
            token = (lax.broadcasted_iota(jnp.int32, (1, size), 1) + start) % TILE
            yrow = jnp.where(start + q_low < 2 * ROWS, ypos, 1 - ypos)
            query = yrow * TILE + token
            key = ypos * TILE + cpos * ASKED + lax.broadcasted_iota(jnp.int32, (ASKED, 1), 0)
            near = jnp.where(key <= query, rest[:ASKED], MASKED)
            rest = jnp.concatenate([near, rest[ASKED:]], axis=0)
        return jnp.concatenate([s[:asked_at] * factor, rest], axis=0)

    def lazy(i, excess):
        start = pl.multiple_of(i * SUB, SUB)
        cols = pl.ds(start, SUB)
        old = pl.ds(pl.multiple_of(start + q_low, 128), SUB)
        s = scores(start, SUB)
        base = m0[:, old]
        p = jnp.exp2(s - base).astype(BF16)
        o = jnp.dot(v_ref[...], p, preferred_element_type=F32)
        m_out[:, cols] = base
        l_out[:, cols] = l0[:, old] + o[HD : HD + 1]
        acc_out[:, cols] = acc0[:, old] + o[:HD]
        return jnp.where(o[HD : HD + 1] <= LIMIT, excess, 1.0)

    excess = lax.fori_loop(0, width // SUB, lazy, jnp.zeros((1, SUB), F32), unroll=min(UNROLL, width // SUB))

    @pl.when(jnp.max(excess) > 0.5)
    def _():
        total = k_ref.shape[0]
        living = jnp.broadcast_to(v_ref[HD:, :].astype(F32)[:1], (128, total)).T

        def exact(i, carry):
            start = pl.multiple_of(i * 128, 128)
            cols = pl.ds(start, 128)
            old = pl.ds(pl.multiple_of(start + q_low, 128), 128)
            s = jnp.where(living > 0.5, scores(start, 128), MASKED)
            base = m0[:, old]
            peak = jnp.maximum(base, jnp.max(s, axis=0, keepdims=True))
            shrink = jnp.exp2(base - peak)
            p = jnp.exp2(s - peak).astype(BF16)
            o = jnp.dot(v_ref[...], p, preferred_element_type=F32)
            m_out[:, cols] = peak
            l_out[:, cols] = l0[:, old] * shrink + o[HD : HD + 1]
            acc_out[:, cols] = acc0[:, old] * shrink + o[:HD]
            return carry

        lax.fori_loop(0, width // 128, exact, 0)

    if mode in ("pack", "only"):
        cols = slice(width - ROWS, width)
        packed_ref[...] = pack(m_out[:, cols], l_out[:, cols], acc_out[:, cols])


def state_shapes(width):
    return [
        jax.ShapeDtypeStruct((1, width), F32),
        jax.ShapeDtypeStruct((1, width), F32),
        jax.ShapeDtypeStruct((HD, width), F32),
    ]


def attend(extent, queries, state, pays, shards, mode, q_low=0, width=BLOCKS * ROWS):
    keys = len(shards) * (KVH * SEND + ASKED + LED)
    scratch = [pltpu.VMEM((keys, HD), BF16), pltpu.VMEM((HD + AUX, keys), BF16)]
    shapes = state_shapes(width)
    if mode == "first":
        args = [extent, *queries, *pays]
        shapes.append(jax.ShapeDtypeStruct((HD + AUX, width), BF16))
        scratch += [pltpu.VMEM((1, width), F32), pltpu.VMEM((1, width), F32), pltpu.VMEM((HD, width), F32)]
    else:
        args = [extent, queries, *state, *pays]
    if mode == "only":
        shapes = []
        scratch += [pltpu.VMEM((1, width), F32), pltpu.VMEM((1, width), F32), pltpu.VMEM((HD, width), F32)]
    if mode in ("pack", "only"):
        shapes.append(jax.ShapeDtypeStruct((HD + AUX, ROWS), BF16))
    vmem = pl.BlockSpec(memory_space=pltpu.VMEM)
    return pl.pallas_call(
        functools.partial(attend_kernel, shards, mode, q_low),
        in_specs=[pl.BlockSpec(memory_space=pltpu.SMEM)] + [vmem] * (len(args) - 1),
        out_specs=[vmem] * len(shapes),
        out_shape=shapes,
        scratch_shapes=scratch,
        compiler_params=params(),
        name="attend",
    )(*args)


def pack(m, l, acc):
    total = m + jnp.log2(l)
    return jnp.concatenate([(acc * (1.0 / l)).astype(BF16), aux_rows(total)], axis=0)


def fold(m, l, acc, received):
    other = join3(received[HD : HD + 3])
    peak = jnp.maximum(m, other)
    mine = jnp.exp2(m - peak)
    theirs = jnp.exp2(other - peak)
    return peak, l * mine + theirs, acc * mine + received[:HD].astype(F32) * theirs


def normal(m, l, acc):
    total = m + jnp.log2(l)
    return total, jnp.ones_like(total), acc * (1.0 / l)


def merge_kernel(m, l, acc, rec, send_ref):
    send_ref[...] = pack(*fold(*normal(m[:, :ROWS], l[:, :ROWS], acc[:, :ROWS]), rec[...]))


def merge_cores(state, received):
    return pl.pallas_call(
        merge_kernel,
        out_shape=jax.ShapeDtypeStruct((HD + AUX, ROWS), BF16),
        compiler_params=params(),
        name="merge",
    )(*state, received)


def finish_kernel(m, l, acc, rec, far, out_ref):
    near = fold(*normal(m[...], l[...], acc[...]), rec[...])
    _, total, summed = fold(*near, far[...])
    result = (summed * (1.0 / total)).astype(BF16)
    tokens, heads, _ = out_ref.shape
    parts = [result[:, h * tokens : (h + 1) * tokens].T for h in range(heads)]
    out_ref[...] = jnp.stack(parts, axis=1)


def finish(state, received, far, shape):
    return pl.pallas_call(
        finish_kernel,
        out_shape=jax.ShapeDtypeStruct(shape, BF16),
        compiler_params=params(),
        name="finish",
    )(*state, received, far)


def body(
    asker_vectors,
    asker_memory_pairs,
    leading_memory_pairs,
    document_memory_pairs,
    document_valid_extent,
    softening_factor,
):
    extent = document_valid_extent
    sending, q0, bare = prepared(extent, softening_factor, document_memory_pairs, asker_vectors)
    q1 = lax.ppermute(bare, "yh", shift(2, 1))
    q2 = lax.ppermute(q0, "c", shift(2, 1))
    moved = lax.all_to_all(sending, ("yl", "x"), 0, 0, tiled=True)
    cache = cache_block(after(asker_memory_pairs, q0), leading_memory_pairs)
    q3 = lax.ppermute(q1, "c", shift(2, 1))
    own = jnp.concatenate([after(moved, q1, q2).reshape(-1, HD), cache], axis=0)

    up, down = shift(RING, 1), shift(RING, -1)
    f1 = lax.ppermute(own, "z", up)
    b1 = lax.ppermute(own, "z", down)
    q0, q2, q1, q3 = lax.optimization_barrier((q0, q2, q1, q3))
    *state, queries = attend(extent, [q0, q2, q1, q3], None, [own], [(0, False)], "first")
    f2 = lax.ppermute(after(f1, state[0]), "z", up)
    b2 = lax.ppermute(after(b1, state[0]), "z", down)
    state = attend(extent, queries, state, [f1, b1], [(-1, False), (1, False)], "middle")
    f3 = lax.ppermute(after(f2, state[0]), "z", up)
    b3 = lax.ppermute(after(b2, state[0]), "z", down)
    state = attend(extent, queries, state, [f2, b2], [(-2, False), (2, False)], "middle")
    f4 = lax.ppermute(after(f3, state[0]), "z", up)
    cross = [(2 * z + y, 2 * ((z - 1) % RING) + 1 - y) for z in range(RING) for y in range(2)]
    b4 = lax.ppermute(after(b3, state[0]), ("z", "yh"), cross)
    half = 2 * ROWS
    last = [(-3, False), (3, False)]
    *apart, packed = attend(extent, queries, state, [f3, b3], last, "pack", half, half)
    received = lax.ppermute(packed, "c", shift(2, 1))
    send = merge_cores(apart, received)
    far = lax.ppermute(send, "yh", shift(2, 1))
    state = attend(extent, queries, state, [after(f3, send), b3], last, "middle", 0, half)
    rest = [(-4, False), (-4, True)]
    (packed,) = attend(extent, queries, state, [f4, b4], rest, "only", ROWS, ROWS)
    received = lax.ppermute(packed, "c", shift(2, 1))
    kept = attend(extent, queries, state, [after(f4, packed), b4], rest, "middle", 0, ROWS)
    return finish(kept, received, far, asker_vectors.shape)


def solution(mesh):
    fine = Mesh(mesh.devices.reshape(8, 2, 2, 4, 2), ("z", "yh", "yl", "x", "c"))
    ctx, head = ("z", "yh"), ("yl", "x", "c")
    return jax.shard_map(
        body,
        mesh=fine,
        in_specs=(
            P(ctx, head, None),
            P(ctx, None, None),
            P(ctx, None, None),
            P(ctx + head, None, None),
            P(),
            P(head),
        ),
        out_specs=P(ctx, head, None),
        check_vma=False,
    )
```
